128 devices in a mesh: row: 4 (over x_hi, core), col: 32 (over z, y, x_lo).
Axes of the slice: x: 4 (x_hi: 2, x_lo: 2; x = x_hi * 2 + x_lo), y: 4, z: 4, core: 2. Of those that a mesh axis runs over, the one named last changes fastest.
Arguments:
- scalar_field: bfloat16 [768, 768, 1024], P('row', 'col'), may hold values from -6 to 6
- x_operator: bfloat16 [1024, 1024], replicated, may hold values from -0.1875 to 0.1875
- y_second: bfloat16 [768, 768], replicated, may hold values from -0.21875 to 0.21875
- y_first: bfloat16 [768, 768], replicated, may hold values from -0.21875 to 0.21875
- y_stretch: float32 [768], replicated, may hold values from 0.5 to 2
- y_curve: float32 [768], replicated, may hold values from -3 to 3
- z_operator: bfloat16 [768, 768], replicated, may hold values from -0.21875 to 0.21875
Outputs:
- diffusion: bfloat16 [768, 768, 1024], P('row', 'col')
The draws below stay inside these ranges and needn't reach their ends.
All inputs are finite; a program needn't handle non-finite values.
Results may differ from the reference program's by a relative error of at most 0.0052.
Values may be sent and summed in bfloat16 or wider, within the bound.
A program may use at most 192 MiB of HBM per device.

```python
import math
import jax
import jax.numpy as jnp
from jax import lax

NX = 1024
NY = 768
NZ = 768
N_COL = 32


def levels(key, shape, pieces, least, largest):
    loudness, own = 1.0, jax.random.fold_in(key, 6)
    for position, blocks in pieces:
        draws = jnp.exp(jax.random.uniform(jax.random.fold_in(own, position), (blocks,), jnp.float32, least / len(pieces), largest / len(pieces)))
        loudness = loudness * jnp.repeat(draws, shape[position] // blocks).reshape([-1 if axis == position else 1 for axis in range(len(shape))])
    return loudness


def scatter_about(own_key, dims, deviation, bound, pieces=(), held_as=jnp.bfloat16):
    loudness = levels(own_key, dims, pieces, -0.22, 0.18) if pieces else 1.0
    values = jax.random.normal(own_key, dims, jnp.float32) * deviation * loudness
    return jnp.minimum(jnp.maximum(values, -bound), bound).astype(held_as)


def setup_inputs(seed: int = 0) -> dict:
    key_of = jax.random.split(jax.random.key(seed), 8)
    scalar_field = scatter_about(key_of[0], (NY, NZ, NX), 1.0, 6.0, ((0, 4), (1, 32)))
    x_operator = scatter_about(key_of[1], (NX, NX), NX ** -0.5, 0.1875)
    y_second = scatter_about(key_of[2], (NY, NY), NY ** -0.5, 0.21875)
    y_first = scatter_about(key_of[3], (NY, NY), NY ** -0.5, 0.21875)
    y_stretch = jnp.clip(jnp.exp(jax.random.uniform(key_of[4], (NY,), jnp.float32, math.log(0.5), math.log(2.0))), 0.5, 2.0)
    y_curve = scatter_about(key_of[5], (NY,), 0.6, 3.0, (), jnp.float32)
    z_operator = scatter_about(key_of[6], (NZ, NZ), NZ ** -0.5, 0.21875)
    return {"scalar_field": scalar_field, "x_operator": x_operator, "y_second": y_second, "y_first": y_first, "y_stretch": y_stretch, "y_curve": y_curve, "z_operator": z_operator}


def reference(scalar_field, x_operator, y_second, y_first, y_stretch, y_curve, z_operator):
    y_combined = (y_stretch[None, :] * y_second.astype(jnp.float32) + y_curve[None, :] * y_first.astype(jnp.float32)).astype(jnp.bfloat16)
    z_blocks = N_COL
    y_size = NY // z_blocks

    def z_apply(planes_in):
        z_full = jnp.einsum('yzx,zk->ykx', planes_in.astype(jnp.float32), z_operator.astype(jnp.float32))
        return z_full.astype(jnp.bfloat16)

    by_rows = scalar_field.reshape(z_blocks, y_size, NZ, NX)
    z_term = lax.map(z_apply, by_rows).reshape(NY, NZ, NX)

    z_size = NZ // z_blocks
    field_cols = jnp.moveaxis(scalar_field.reshape(NY, z_blocks, z_size, NX), 1, 0)
    zterm_cols = jnp.moveaxis(z_term.reshape(NY, z_blocks, z_size, NX), 1, 0)

    def combine(inputs):
        column_in, z_part = inputs
        x_term = jnp.einsum('yzx,xk->yzk', column_in.astype(jnp.float32), x_operator.astype(jnp.float32))
        y_term = jnp.einsum('yzx,yk->kzx', column_in.astype(jnp.float32), y_combined.astype(jnp.float32)).astype(jnp.bfloat16)
        total = x_term + y_term.astype(jnp.float32) + z_part.astype(jnp.float32)
        return total.astype(jnp.bfloat16)

    result = lax.map(combine, (field_cols, zterm_cols))
    return jnp.moveaxis(result, 0, 1).reshape(NY, NZ, NX)
```

```python
import functools

import jax
import jax.numpy as jnp
from jax import lax
from jax.experimental import pallas as pl
from jax.experimental.pallas import tpu as pltpu
from jax.sharding import PartitionSpec as P

MESH = pl.DeviceIdType.MESH
BF16 = jnp.bfloat16
F32 = jnp.float32
LANES = 128
CHUNKS = 4
PLANE = 16
ROWS = 192
ZS = 24
YS = ROWS // PLANE
HALF = ZS // 2
NY = 4 * ROWS
NZ = 2 * PLANE * ZS


def exchange_kernel(
    field, y_op, z_op,
    total, traded, z_in, y_in, z_out,
    turn, staged, block, z_pencil, z_result, y_pencil, y_send, y_own, y_got, z_got, summed,
    lo_s, lo_r, zi_s, zi_r, g_s, g_l, g_r, zo_s, zo_l, zo_r, ys_s, ys_r, back_s, back_r, keep_l, load,
):
    row, col = lax.axis_index("row"), lax.axis_index("col")
    hi, core = row // 2, row % 2
    plane, lo = col // 2, col % 2
    pz, py = plane // 4, plane % 4
    upper = 1 - lax.rem(hi + lo, 2)
    mine, theirs = upper * (CHUNKS * LANES), (1 - upper) * (CHUNKS * LANES)
    other_lo = 1 - lo

    lo_peer = (row, plane * 2 + other_lo)
    sibling = (hi * 2 + 1 - core, col)
    far_same = ((1 - hi) * 2 + core, plane * 2 + other_lo)
    far_cross = ((1 - hi) * 2 + 1 - core, plane * 2 + other_lo)

    def plane_peer(k):
        return lax.rem(pz + k // 4, 4) * 4 + lax.rem(py + k % 4, 4)

    def lanes(start, i):
        return pl.ds(pl.multiple_of(start + i * LANES, LANES), LANES)

    def remote(src, dst, send, recv, device):
        return pltpu.make_async_remote_copy(
            src_ref=src, dst_ref=dst, send_sem=send, recv_sem=recv, device_id=device, device_id_type=MESH
        )

    def drain(ref, sem):
        pltpu.make_async_copy(ref, ref, sem).wait()

    def fetch(src, dst):
        copy = pltpu.make_async_copy(src, dst, load)
        copy.start()
        copy.wait()

    barrier = pltpu.get_barrier_semaphore()
    for peer in (lo_peer, sibling, far_same, far_cross):
        pl.semaphore_signal(barrier, inc=1, device_id=peer, device_id_type=MESH)

    @pl.loop(1, PLANE)
    def _(k):
        pl.semaphore_signal(barrier, inc=1, device_id=(row, plane_peer(k) * 2 + lo), device_id_type=MESH)

    pl.semaphore_wait(barrier, 4 + PLANE - 1)

    def part_of(i, own):
        return field.at[:, :, lanes(mine, i)] if own else traded.at[i]

    def send_z(i, own):
        source = part_of(i, own)
        z_half = lo if own else other_lo
        part = 0 if own else 1

        @pl.loop(1, PLANE)
        def _(k):
            to = plane_peer(k)
            remote(
                source.at[pl.ds(to * YS, YS)], z_in.at[i, :, plane, z_half],
                zi_s.at[i, part], zi_r.at[i], (row, to * 2 + lo),
            ).start()

        pltpu.make_async_copy(
            source.at[pl.ds(plane * YS, YS)], z_in.at[i, :, plane, z_half], zi_r.at[i]
        ).start()

    def send_y(i, own):
        part, z_half = (0, lo) if own else (1, other_lo)
        if not own:
            drain(staged.at[i, pl.ds(0, HALF)], g_l.at[i, 0])
            for n in range(3):
                drain(staged.at[i, pl.ds(0, HALF)], g_s.at[i, 0, n])
        fetch(part_of(i, own), block)

        @pl.loop(0, ROWS // 16)
        def _(j):
            turn[pl.ds(j * 16 * ZS, 16 * ZS)] = block[pl.ds(j * 16, 16)].astype(F32).reshape(16 * ZS, LANES)

        @pl.loop(0, ZS)
        def _(z):
            staged[i, z] = turn[pl.ds(z, ROWS, stride=ZS)].astype(BF16)

        keep, give = pl.ds(core * HALF, HALF), pl.ds((1 - core) * HALF, HALF)
        for n, (piece, peer) in enumerate(((keep, far_same), (give, far_cross), (give, sibling))):
            remote(
                staged.at[i, piece], y_in.at[i, z_half, :, row], g_s.at[i, part, n], g_r.at[i, z_half], peer
            ).start()
        pltpu.make_async_copy(staged.at[i, keep], y_in.at[i, z_half, :, row], g_l.at[i, part]).start()

    def do_z(i):
        slot = i % 2
        if i >= 2:
            for half in range(2):
                drain(z_out.at[i, half, pl.ds(0, YS)], zo_l.at[i - 2, half])
                drain(z_out.at[i, half, pl.ds(0, (PLANE - 1) * YS)], zo_s.at[i - 2, half])
        drain(z_in.at[i], zi_r.at[i])
        fetch(z_in.at[i], z_pencil)

        @pl.loop(0, YS // 2)
        def _(j):
            def points(y):
                return z_pencil[y].astype(F32).reshape(NZ, LANES).astype(BF16)

            pair = jnp.concatenate([points(2 * j), points(2 * j + 1)], axis=1)
            product = jnp.dot(z_op[...], pair, preferred_element_type=F32)
            for n in range(2):
                result = product[:, n * LANES:(n + 1) * LANES].reshape(PLANE, 2, ZS, LANES)
                z_result[slot, 2 * j + n] = result.astype(BF16)

        for half in (other_lo, lo):
            @pl.loop(1, PLANE)
            def _(k):
                to = plane_peer(k)
                remote(
                    z_result.at[slot, :, to, half], z_out.at[i, half, pl.ds(plane * YS, YS)],
                    zo_s.at[i, half], zo_r.at[i, half], (row, to * 2 + lo),
                ).start()

            pltpu.make_async_copy(
                z_result.at[slot, :, plane, half], z_out.at[i, half, pl.ds(plane * YS, YS)], zo_l.at[i, half]
            ).start()

    def do_y(i, own):
        part, half = (0, lo) if own else (1, other_lo)
        drain(y_in.at[i, half, :, pl.ds(0, 3)], g_r.at[i, half])
        if not own:
            drain(staged.at[i, pl.ds(0, HALF)], g_l.at[i, 1])
        fetch(y_in.at[i, half], y_pencil)

        @pl.loop(0, HALF // 2)
        def _(j):
            pair = jnp.concatenate(
                [y_pencil[2 * j].reshape(NY, LANES), y_pencil[2 * j + 1].reshape(NY, LANES)], axis=1
            )
            product = jnp.dot(y_op[...], pair, preferred_element_type=F32).astype(BF16)
            for n in range(2):
                y_own[i, part, 2 * j + n] = product[:ROWS, n * LANES:(n + 1) * LANES]
                y_send[i, part, 2 * j + n] = product[ROWS:, n * LANES:(n + 1) * LANES]

        remote(y_send.at[i, part], y_got.at[i, part], ys_s.at[i, part], ys_r.at[i, part], sibling).start()

    def combine(i, own):
        part, half = (0, lo) if own else (1, other_lo)
        drain(y_got.at[i, part], ys_r.at[i, part])
        drain(z_out.at[i, half, pl.ds(0, (PLANE - 1) * YS)], zo_r.at[i, half])
        if i >= 2:
            drain(z_out.at[i, half, pl.ds(0, YS)], zo_l.at[i, half])
        fetch(z_out.at[i, half], z_got)

        @pl.loop(0, HALF)
        def _(z):
            turn[pl.ds(core * HALF + z, ROWS, stride=ZS)] = y_own[i, part, z].astype(F32)
            turn[pl.ds((1 - core) * HALF + z, ROWS, stride=ZS)] = y_got[i, part, z].astype(F32)

        if own:
            drain(summed.at[i], back_s.at[i])

        @pl.loop(0, ROWS // 16)
        def _(j):
            rows = pl.ds(j * 16, 16)
            y_term = turn[pl.ds(j * 16 * ZS, 16 * ZS)].reshape(16, ZS, LANES)
            summed[i, rows] = (y_term + z_got[rows].astype(F32)).astype(BF16)

        if own:
            pltpu.make_async_copy(summed.at[i], total.at[:, :, lanes(mine, i)], keep_l.at[i]).start()
        else:
            remote(summed.at[i], total.at[:, :, lanes(mine, i)], back_s.at[i], back_r.at[i], lo_peer).start()

    def take(i):
        drain(traded.at[i], lo_r.at[i])
        send_z(i, False)
        send_y(i, False)

    for i in range(CHUNKS):
        remote(field.at[:, :, lanes(theirs, i)], traded.at[i], lo_s.at[i], lo_r.at[i], lo_peer).start()
        send_z(i, True)
        send_y(i, True)
    take(0)
    take(1)
    do_z(0)
    take(2)
    do_z(1)
    take(3)
    for i in range(CHUNKS):
        do_y(i, False)
        if i < 2:
            do_z(i + 2)
        combine(i, False)
    for i in range(CHUNKS):
        do_y(i, True)
        combine(i, True)

    for i in range(CHUNKS):
        drain(traded.at[i], lo_s.at[i])
        for part in range(2):
            drain(z_in.at[i, :, pl.ds(0, PLANE - 1), 0], zi_s.at[i, part])
            drain(y_send.at[i, part], ys_s.at[i, part])
        for n in range(3):
            drain(staged.at[i, pl.ds(0, HALF)], g_s.at[i, 1, n])
        if i >= 2:
            for half in range(2):
                drain(z_out.at[i, half, pl.ds(0, (PLANE - 1) * YS)], zo_s.at[i, half])
        drain(summed.at[i], keep_l.at[i])
        drain(summed.at[i], back_r.at[i])


def exchange(field, y_op, z_op):
    any_space, vmem = pl.BlockSpec(memory_space=pl.ANY), pl.BlockSpec(memory_space=pltpu.VMEM)
    shape = lambda *dims: jax.ShapeDtypeStruct(dims, BF16)
    dma = pltpu.SemaphoreType.DMA
    return pl.pallas_call(
        exchange_kernel,
        name="exchange",
        out_shape=(
            shape(ROWS, ZS, 2 * CHUNKS * LANES),
            shape(CHUNKS, ROWS, ZS, LANES),
            shape(CHUNKS, YS, PLANE, 2, ZS, LANES),
            shape(CHUNKS, 2, HALF, 4, ROWS, LANES),
            shape(CHUNKS, 2, ROWS, ZS, LANES),
        ),
        in_specs=[any_space, vmem, vmem],
        out_specs=(any_space,) * 5,
        scratch_shapes=[
            pltpu.VMEM((ROWS * ZS, LANES), F32),
            pltpu.VMEM((CHUNKS, ZS, ROWS, LANES), BF16),
            pltpu.VMEM((ROWS, ZS, LANES), BF16),
            pltpu.VMEM((YS, PLANE, 2, ZS, LANES), BF16),
            pltpu.VMEM((2, YS, PLANE, 2, ZS, LANES), BF16),
            pltpu.VMEM((HALF, 4, ROWS, LANES), BF16),
            pltpu.VMEM((CHUNKS, 2, HALF, ROWS, LANES), BF16),
            pltpu.VMEM((CHUNKS, 2, HALF, ROWS, LANES), BF16),
            pltpu.VMEM((CHUNKS, 2, HALF, ROWS, LANES), BF16),
            pltpu.VMEM((ROWS, ZS, LANES), BF16),
            pltpu.VMEM((CHUNKS, ROWS, ZS, LANES), BF16),
            dma((CHUNKS,)), dma((CHUNKS,)),
            dma((CHUNKS, 2)), dma((CHUNKS,)),
            dma((CHUNKS, 2, 3)), dma((CHUNKS, 2)), dma((CHUNKS, 2)),
            dma((CHUNKS, 2)), dma((CHUNKS, 2)), dma((CHUNKS, 2)),
            dma((CHUNKS, 2)), dma((CHUNKS, 2)),
            dma((CHUNKS,)), dma((CHUNKS,)),
            dma((CHUNKS,)), dma,
        ],
        compiler_params=pltpu.CompilerParams(
            collective_id=0, has_side_effects=True, vmem_limit_bytes=58 * 2**20
        ),
        cost_estimate=pl.CostEstimate(flops=14_500_000_000, bytes_accessed=100_000_000, transcendentals=0),
    )(field, y_op, z_op)[0]


def x_kernel(field, x_op, rest, out):
    rows = field.shape[0] * field.shape[1]
    flat = field[...].reshape(rows, field.shape[2])
    product = jnp.dot(flat, x_op[...], preferred_element_type=F32)
    out[...] = (product.reshape(out.shape) + rest[...].astype(F32)).astype(BF16)


def add_x(field, x_op, rest):
    nx = field.shape[2]
    step = 16
    tile = pl.BlockSpec((step, ZS, nx), lambda i: (i, 0, 0))
    return pl.pallas_call(
        x_kernel,
        name="x_term",
        grid=(ROWS // step,),
        in_specs=[tile, pl.BlockSpec((nx, nx), lambda i: (0, 0)), tile],
        out_specs=tile,
        out_shape=jax.ShapeDtypeStruct(field.shape, BF16),
        compiler_params=pltpu.CompilerParams(vmem_limit_bytes=48 * 2**20),
    )(field, x_op, rest)


def per_device(scalar_field, x_operator, y_second, y_first, y_stretch, y_curve, z_operator):
    row = lax.axis_index("row")

    def operator_rows(r):
        cut = lambda a, axis: lax.dynamic_slice_in_dim(a, r * ROWS, ROWS, axis)
        return (
            cut(y_stretch, 0)[None, :] * cut(y_second, 1).astype(F32)
            + cut(y_curve, 0)[None, :] * cut(y_first, 1).astype(F32)
        ).astype(BF16).T

    sibling = row + 1 - 2 * lax.rem(row, 2)
    y_op = jnp.concatenate([operator_rows(row), operator_rows(sibling)], axis=0)
    rest = exchange(scalar_field, y_op, z_operator.T)
    return add_x(scalar_field, x_operator, rest)


def solution(mesh):
    in_specs = (P("row", "col", None), P(), P(), P(), P(), P(), P())
    out_specs = P("row", "col", None)
    return jax.shard_map(
        per_device, mesh=mesh, in_specs=in_specs, out_specs=out_specs, check_vma=False
    )
```

```python
import jax
import jax.numpy as jnp
from jax import lax
from jax.experimental import pallas as pl
from jax.experimental.pallas import tpu as pltpu
from jax.sharding import PartitionSpec as P

MESH = pl.DeviceIdType.MESH
BF16 = jnp.bfloat16
F32 = jnp.float32
LANES = 128
CHUNKS = 4
PLANE = 16
ROWS = 192
ZS = 24
YS = ROWS // PLANE
HALF = ZS // 2
XS = 16
NY = 4 * ROWS
NZ = 2 * PLANE * ZS


def laplacian_kernel(
    field, x_source, y_second, y_first, y_stretch, y_curve, z_source,
    total, traded, z_in, y_in, z_out, back, x_term,
    x_op, y_parts, y_op, z_raw, z_op, x_tile, x_result, x_got,
    turn, staged, block, z_pencil, z_result, y_pencil, y_result, y_got, z_got, summed, final,
    lo_s, lo_r, zi_s, zi_r, g_s, g_l, g_r, zo_s, zo_r, ys_s, ys_r, back_s, back_r, keep_l, load, ops_l, x_l, x_s,
    x_g,
):
    row, col = lax.axis_index("row"), lax.axis_index("col")
    hi, core = row // 2, row % 2
    plane, lo = col // 2, col % 2
    pz, py = plane // 4, plane % 4
    upper = 1 - lax.rem(hi + lo, 2)
    mine, theirs = upper * (CHUNKS * LANES), (1 - upper) * (CHUNKS * LANES)
    other_lo = 1 - lo

    lo_peer = (row, plane * 2 + other_lo)
    sibling = (hi * 2 + 1 - core, col)
    far_same = ((1 - hi) * 2 + core, plane * 2 + other_lo)
    far_cross = ((1 - hi) * 2 + 1 - core, plane * 2 + other_lo)

    def plane_peer(k):
        k = lax.rem(k * 7, PLANE)
        return lax.rem(pz + k // 4, 4) * 4 + lax.rem(py + k % 4, 4)

    def lanes(start, i):
        return pl.ds(pl.multiple_of(start + i * LANES, LANES), LANES)

    def remote(src, dst, send, recv, device):
        return pltpu.make_async_remote_copy(
            src_ref=src, dst_ref=dst, send_sem=send, recv_sem=recv, device_id=device, device_id_type=MESH
        )

    def drain(ref, sem):
        pltpu.make_async_copy(ref, ref, sem).wait()

    def fetch(src, dst):
        copy = pltpu.make_async_copy(src, dst, load)
        copy.start()
        copy.wait()

    y_columns = pl.ds(pl.multiple_of(hi * (2 * ROWS), LANES), 2 * ROWS)
    loads = [
        pltpu.make_async_copy(source, target, ops_l.at[n])
        for n, (source, target) in enumerate((
            (x_source, x_op), (y_second.at[:, y_columns], y_parts.at[0]),
            (y_first.at[:, y_columns], y_parts.at[1]), (z_source, z_raw),
        ))
    ]
    for copy in loads:
        copy.start()

    barrier = pltpu.get_barrier_semaphore()
    for peer in (lo_peer, sibling, far_same, far_cross):
        pl.semaphore_signal(barrier, inc=1, device_id=peer, device_id_type=MESH)

    @pl.loop(1, PLANE)
    def _(k):
        pl.semaphore_signal(barrier, inc=1, device_id=(row, plane_peer(k) * 2 + lo), device_id_type=MESH)

    pl.semaphore_wait(barrier, 4 + PLANE - 1)

    def part_of(i, own):
        return field.at[:, :, lanes(mine, i)] if own else traded.at[i]

    def send_z(i, own):
        source = part_of(i, own)
        z_half = lo if own else other_lo
        part = 0 if own else 1

        @pl.loop(1, PLANE)
        def _(k):
            to = plane_peer(k)
            remote(
                source.at[pl.ds(to * YS, YS)], z_in.at[i, :, plane, z_half],
                zi_s.at[i, part], zi_r.at[i], (row, to * 2 + lo),
            ).start()

        pltpu.make_async_copy(
            source.at[pl.ds(plane * YS, YS)], z_in.at[i, :, plane, z_half], zi_r.at[i]
        ).start()

    def send_y(i, own):
        part, z_half = (0, lo) if own else (1, other_lo)
        if not own:
            drain(staged.at[i, pl.ds(0, HALF)], g_l.at[i, 0])
            for n in range(3):
                drain(staged.at[i, pl.ds(0, HALF)], g_s.at[i, 0, n])
        fetch(part_of(i, own), block)

        @pl.loop(0, ROWS // 16)
        def _(j):
            turn[pl.ds(j * 16 * ZS, 16 * ZS)] = block[pl.ds(j * 16, 16)].astype(F32).reshape(16 * ZS, LANES)

        @pl.loop(0, ZS)
        def _(z):
            staged[i, z] = turn[pl.ds(z, ROWS, stride=ZS)].astype(BF16)

        keep, give = pl.ds(core * HALF, HALF), pl.ds((1 - core) * HALF, HALF)
        for n, (piece, peer) in enumerate(((keep, far_same), (give, far_cross), (give, sibling))):
            remote(
                staged.at[i, piece], y_in.at[i, z_half, :, row], g_s.at[i, part, n], g_r.at[i, z_half], peer
            ).start()
        pltpu.make_async_copy(staged.at[i, keep], y_in.at[i, z_half, :, row], g_l.at[i, part]).start()

    def do_z(i):
        drain(z_in.at[i], zi_r.at[i])
        fetch(z_in.at[i], z_pencil)

        @pl.loop(0, YS // 2)
        def _(j):
            def points(y):
                return z_pencil[y].astype(F32).reshape(NZ, LANES).astype(BF16)

            pair = jnp.concatenate([points(2 * j), points(2 * j + 1)], axis=1)
            product = jnp.dot(z_op[...], pair, preferred_element_type=F32)
            for n in range(2):
                result = product[:, n * LANES:(n + 1) * LANES].reshape(PLANE, 2, ZS, LANES)
                z_result[i, 2 * j + n] = result.astype(BF16)

    def return_z(i, own):
        half = lo if own else other_lo

        @pl.loop(1, PLANE)
        def _(k):
            to = plane_peer(k)
            remote(
                z_result.at[i, :, to, half], z_out.at[i, half, pl.ds(plane * YS, YS)],
                zo_s.at[i, half], zo_r.at[i, half], (row, to * 2 + lo),
            ).start()

        pltpu.make_async_copy(
            z_result.at[i, :, plane, half], z_out.at[i, half, pl.ds(plane * YS, YS)], zo_r.at[i, half]
        ).start()

    def make_y_op():
        loads[1].wait()
        loads[2].wait()
        for n in range(3):
            here = slice(n * LANES, (n + 1) * LANES)
            there = pl.ds(pl.multiple_of(hi * (2 * ROWS) + n * LANES, LANES), LANES)
            combined = (
                y_stretch[:, there] * y_parts[0, :, here].astype(F32)
                + y_curve[:, there] * y_parts[1, :, here].astype(F32)
            )
            y_op[here] = combined.T.astype(BF16)

    def make_z_op():
        loads[3].wait()
        for n in range(NZ // LANES):
            here = slice(n * LANES, (n + 1) * LANES)
            z_op[here] = z_raw[:, here].astype(F32).T.astype(BF16)

    def x_load(j, slot):
        return pltpu.make_async_copy(field.at[pl.ds(j * XS, XS)], x_tile.at[slot], x_l.at[slot])

    def x_store(j, slot):
        return pltpu.make_async_copy(x_result.at[slot], x_term.at[:, pl.ds(j * XS, XS)], x_s.at[slot])

    def do_x(first, last):
        @pl.loop(first, last)
        def _(j):
            slot = lax.rem(j, 2)
            x_load(j, slot).wait()

            @pl.when(j + 1 < ROWS // XS)
            def _():
                x_load(j + 1, 1 - slot).start()

            @pl.when(j >= 2)
            def _():
                x_store(j - 2, slot).wait()

            flat = x_tile[slot].reshape(XS * ZS, 2 * CHUNKS * LANES)
            product = jnp.dot(flat, x_op[...], preferred_element_type=F32)
            for n in range(2 * CHUNKS):
                x_result[slot, n] = product[:, n * LANES:(n + 1) * LANES].reshape(XS, ZS, LANES)
            x_store(j, slot).start()

    def do_y(i, own):
        part, half = (0, lo) if own else (1, other_lo)
        drain(y_in.at[i, half, :, pl.ds(0, 3)], g_r.at[i, half])
        if not own:
            drain(staged.at[i, pl.ds(0, HALF)], g_l.at[i, 1])
        fetch(y_in.at[i, half], y_pencil)

        @pl.loop(0, HALF // 2)
        def _(j):
            pair = jnp.concatenate(
                [y_pencil[2 * j].reshape(NY, LANES), y_pencil[2 * j + 1].reshape(NY, LANES)], axis=1
            )
            product = jnp.dot(y_op[...], pair, preferred_element_type=F32).astype(BF16)
            for n in range(2):
                for c in range(2):
                    y_result[i, part, c, 2 * j + n] = product[c * ROWS:(c + 1) * ROWS, n * LANES:(n + 1) * LANES]

        remote(
            y_result.at[i, part, 1 - core], y_got.at[i, part], ys_s.at[i, part], ys_r.at[i, part], sibling
        ).start()

    def x_fetch(i, own):
        return pltpu.make_async_copy(x_term.at[(upper if own else 1 - upper) * CHUNKS + i], x_got, x_g)

    order = [(0, False), (1, False), (0, True), (2, False), (1, True), (2, True), (3, False), (3, True)]

    def keep(i, own):
        n = order.index((i, own)) % 2
        return pltpu.make_async_copy(
            final.at[n], total.at[:, :, lanes(mine if own else theirs, i)], keep_l.at[n]
        )

    def slot_for(i, own):
        n = order.index((i, own))
        if n >= 2:
            keep(*order[n - 2]).wait()
        return n % 2

    def combine(i, own):
        part, half = (0, lo) if own else (1, other_lo)
        if own:
            x_fetch(i, True).start()
        drain(y_got.at[i, part], ys_r.at[i, part])

        @pl.loop(0, HALF)
        def _(z):
            turn[pl.ds(core * HALF + z, ROWS, stride=ZS)] = y_result[i, part, core, z].astype(F32)
            turn[pl.ds((1 - core) * HALF + z, ROWS, stride=ZS)] = y_got[i, part, z].astype(F32)

        drain(z_out.at[i, half], zo_r.at[i, half])
        fetch(z_out.at[i, half], z_got)
        if own:
            x_fetch(i, True).wait()
            slot = slot_for(i, True)

        @pl.loop(0, ROWS // 16)
        def _(j):
            rows = pl.ds(j * 16, 16)
            both = turn[pl.ds(j * 16 * ZS, 16 * ZS)].reshape(16, ZS, LANES) + z_got[rows].astype(F32)
            if own:
                final[slot, rows] = (both + x_got[rows]).astype(BF16)
            else:
                summed[i, rows] = both.astype(BF16)

        if own:
            keep(i, True).start()
        else:
            remote(summed.at[i], back.at[i], back_s.at[i], back_r.at[i], lo_peer).start()

    def finish(i):
        x_fetch(i, False).start()
        drain(back.at[i], back_r.at[i])
        fetch(back.at[i], z_got)
        x_fetch(i, False).wait()
        slot = slot_for(i, False)

        @pl.loop(0, ROWS // 16)
        def _(j):
            rows = pl.ds(j * 16, 16)
            final[slot, rows] = (z_got[rows].astype(F32) + x_got[rows]).astype(BF16)

        keep(i, False).start()

    def take(i):
        drain(traded.at[i], lo_r.at[i])
        send_z(i, False)
        send_y(i, False)

    for i in range(CHUNKS):
        remote(field.at[:, :, lanes(theirs, i)], traded.at[i], lo_s.at[i], lo_r.at[i], lo_peer).start()
    x_load(0, 0).start()
    send_z(0, True)
    send_y(0, True)
    send_z(1, True)
    send_z(2, True)
    for i in range(1, CHUNKS):
        send_y(i, True)
    loads[0].wait()
    do_x(0, 6)
    take(0)
    make_y_op()
    make_z_op()
    do_y(0, False)
    do_x(6, 12)
    for slot in range(2):
        x_store(slot, slot).wait()
    take(1)
    do_z(0)
    return_z(0, False)
    send_z(3, True)
    do_y(1, False)
    take(2)
    do_z(1)
    return_z(1, False)
    combine(0, False)
    do_y(2, False)
    take(3)
    do_z(2)
    return_z(2, False)
    combine(1, False)
    do_z(3)
    return_z(3, False)
    for i in range(CHUNKS):
        return_z(i, True)
    do_y(3, False)
    finish(0)
    do_y(0, True)
    combine(2, False)
    combine(3, False)
    finish(1)
    do_y(1, True)
    combine(0, True)
    finish(2)
    do_y(2, True)
    combine(1, True)
    combine(2, True)
    do_y(3, True)
    finish(3)
    combine(3, True)

    for i in range(CHUNKS):
        drain(traded.at[i], lo_s.at[i])
        for part in range(2):
            drain(z_in.at[i, :, pl.ds(0, PLANE - 1), 0], zi_s.at[i, part])
            drain(y_got.at[i, part], ys_s.at[i, part])
        for n in range(3):
            drain(staged.at[i, pl.ds(0, HALF)], g_s.at[i, 1, n])
        for half in range(2):
            drain(z_out.at[i, half, pl.ds(0, (PLANE - 1) * YS)], zo_s.at[i, half])
        drain(summed.at[i], back_s.at[i])
    for block_id in order[-2:]:
        keep(*block_id).wait()


def laplacian(*operands):
    any_space, vmem = pl.BlockSpec(memory_space=pl.ANY), pl.BlockSpec(memory_space=pltpu.VMEM)
    shape = lambda *dims: jax.ShapeDtypeStruct(dims, BF16)
    held = lambda *dims: pltpu.VMEM(dims, BF16)
    dma = pltpu.SemaphoreType.DMA
    nx = 2 * CHUNKS * LANES
    return pl.pallas_call(
        laplacian_kernel,
        name="laplacian",
        out_shape=(
            shape(ROWS, ZS, nx),
            shape(CHUNKS, ROWS, ZS, LANES),
            shape(CHUNKS, YS, PLANE, 2, ZS, LANES),
            shape(CHUNKS, 2, HALF, 4, ROWS, LANES),
            shape(CHUNKS, 2, ROWS, ZS, LANES),
            shape(CHUNKS, ROWS, ZS, LANES),
            jax.ShapeDtypeStruct((2 * CHUNKS, ROWS, ZS, LANES), F32),
        ),
        in_specs=[any_space] * 4 + [vmem] * 2 + [any_space],
        out_specs=(any_space,) * 7,
        scratch_shapes=[
            held(nx, nx), held(2, NY, 2 * ROWS), held(2 * ROWS, NY), held(NZ, NZ), held(NZ, NZ),
            held(2, XS, ZS, nx),
            pltpu.VMEM((2, 2 * CHUNKS, XS, ZS, LANES), F32),
            pltpu.VMEM((ROWS, ZS, LANES), F32),
            pltpu.VMEM((ROWS * ZS, LANES), F32),
            held(CHUNKS, ZS, ROWS, LANES),
            held(ROWS, ZS, LANES),
            held(YS, PLANE, 2, ZS, LANES),
            held(CHUNKS, YS, PLANE, 2, ZS, LANES),
            held(HALF, 4, ROWS, LANES),
            held(CHUNKS, 2, 2, HALF, ROWS, LANES),
            held(CHUNKS, 2, HALF, ROWS, LANES),
            held(ROWS, ZS, LANES),
            held(CHUNKS, ROWS, ZS, LANES),
            held(2, ROWS, ZS, LANES),
            dma((CHUNKS,)), dma((CHUNKS,)),
            dma((CHUNKS, 2)), dma((CHUNKS,)),
            dma((CHUNKS, 2, 3)), dma((CHUNKS, 2)), dma((CHUNKS, 2)),
            dma((CHUNKS, 2)), dma((CHUNKS, 2)),
            dma((CHUNKS, 2)), dma((CHUNKS, 2)),
            dma((CHUNKS,)), dma((CHUNKS,)),
            dma((2,)), dma, dma((4,)), dma((2,)), dma((2,)), dma,
        ],
        compiler_params=pltpu.CompilerParams(
            collective_id=0, has_side_effects=True, vmem_limit_bytes=62 * 2**20
        ),
        cost_estimate=pl.CostEstimate(flops=24_200_000_000, bytes_accessed=180_000_000, transcendentals=0),
    )(*operands)[0]


def copy_kernel(source, target, held, read, written):
    parts = read.shape[0]
    rows = source.shape[0] // parts
    piece = lambda n: pl.ds(n * rows, rows)
    reads = [pltpu.make_async_copy(source.at[piece(n)], held.at[piece(n)], read.at[n]) for n in range(parts)]
    writes = [pltpu.make_async_copy(held.at[piece(n)], target.at[piece(n)], written.at[n]) for n in range(parts)]
    for copy in reads:
        copy.start()
    for n in range(parts):
        reads[n].wait()
        writes[n].start()
    for copy in writes:
        copy.wait()


def copied(array):
    any_space = pl.BlockSpec(memory_space=pl.ANY)
    parts = 12
    return pl.pallas_call(
        copy_kernel,
        name="result",
        in_specs=[any_space],
        out_specs=any_space,
        out_shape=jax.ShapeDtypeStruct(array.shape, array.dtype),
        scratch_shapes=[
            pltpu.VMEM(array.shape, array.dtype),
            pltpu.SemaphoreType.DMA((parts,)), pltpu.SemaphoreType.DMA((parts,)),
        ],
        compiler_params=pltpu.CompilerParams(vmem_limit_bytes=60 * 2**20),
    )(array)


def per_device(scalar_field, x_operator, y_second, y_first, y_stretch, y_curve, z_operator):
    return copied(laplacian(
        scalar_field, x_operator, y_second, y_first, y_stretch[None, :], y_curve[None, :], z_operator
    ))


def solution(mesh):
    in_specs = (P("row", "col", None), P(), P(), P(), P(), P(), P())
    out_specs = P("row", "col", None)
    return jax.shard_map(
        per_device, mesh=mesh, in_specs=in_specs, out_specs=out_specs, check_vma=False
    )
```

```python
import jax
import jax.numpy as jnp
from jax import lax
from jax.experimental import pallas as pl
from jax.experimental.pallas import tpu as pltpu
from jax.sharding import PartitionSpec as P

MESH = pl.DeviceIdType.MESH
BF16 = jnp.bfloat16
F32 = jnp.float32
LANES = 128
CHUNKS = 4
PLANE = 16
ROWS = 192
ZS = 24
YS = ROWS // PLANE
HALF = ZS // 2
QUARTER = HALF // 2
LAST = CHUNKS - 1
XS = 8
NY = 4 * ROWS
NZ = 2 * PLANE * ZS


def laplacian_kernel(
    field, x_source, y_second, y_first, y_stretch, y_curve, z_source,
    total, traded, z_in, y_in, z_out, x_term,
    x_op, y_parts, y_op, z_raw, z_op, x_tile, x_result, x_got,
    turn, staged, block, z_pencil, z_result, y_pencil, y_result, y_got, z_got, summed, final,
    back, y_last, z_last,
    lo_s, lo_r, zi_s, zi_r, g_s, g_l, g_r, zo_s, zo_r, ys_s, ys_r, back_s, back_r, keep_l, load, ops_l, x_l, x_s,
    x_g, z_l, last_r, last_ys_s, last_ys_r,
):
    row, col = lax.axis_index("row"), lax.axis_index("col")
    hi, core = row // 2, row % 2
    plane, lo = col // 2, col % 2
    pz, py = plane // 4, plane % 4
    upper = 1 - lax.rem(hi + lo, 2)
    mine, theirs = upper * (CHUNKS * LANES), (1 - upper) * (CHUNKS * LANES)
    other_lo = 1 - lo

    lo_peer = (row, plane * 2 + other_lo)
    sibling = (hi * 2 + 1 - core, col)
    far_same = ((1 - hi) * 2 + core, plane * 2 + other_lo)
    far_cross = ((1 - hi) * 2 + 1 - core, plane * 2 + other_lo)

    def plane_peer(k):
        k = lax.rem(k * 7, PLANE)
        return lax.rem(pz + k // 4, 4) * 4 + lax.rem(py + k % 4, 4)

    def lanes(start, i):
        return pl.ds(pl.multiple_of(start + i * LANES, LANES), LANES)

    def remote(src, dst, send, recv, device):
        return pltpu.make_async_remote_copy(
            src_ref=src, dst_ref=dst, send_sem=send, recv_sem=recv, device_id=device, device_id_type=MESH
        )

    def drain(ref, sem):
        pltpu.make_async_copy(ref, ref, sem).wait()

    def fetch(src, dst):
        copy = pltpu.make_async_copy(src, dst, load)
        copy.start()
        copy.wait()

    y_columns = pl.ds(pl.multiple_of(hi * (2 * ROWS), LANES), 2 * ROWS)
    loads = [
        pltpu.make_async_copy(source, target, ops_l.at[n])
        for n, (source, target) in enumerate((
            (x_source, x_op), (y_second.at[:, y_columns], y_parts.at[0]),
            (y_first.at[:, y_columns], y_parts.at[1]), (z_source, z_raw),
        ))
    ]
    for copy in loads:
        copy.start()

    def x_load(j, slot):
        return pltpu.make_async_copy(field.at[pl.ds(j * XS, XS)], x_tile.at[slot], x_l.at[slot])

    barrier = pltpu.get_barrier_semaphore()
    for peer in (lo_peer, sibling, far_same, far_cross):
        pl.semaphore_signal(barrier, inc=1, device_id=peer, device_id_type=MESH)

    @pl.loop(1, PLANE)
    def _(k):
        pl.semaphore_signal(barrier, inc=1, device_id=(row, plane_peer(k) * 2 + lo), device_id_type=MESH)

    first_block = pltpu.make_async_copy(field.at[:, :, lanes(mine, 0)], block, load)
    first_block.start()
    x_load(0, 0).start()
    pl.semaphore_wait(barrier, 4 + PLANE - 1)

    def part_of(i, own):
        return field.at[:, :, lanes(mine, i)] if own else traded.at[i]

    def send_z(i, own):
        source = part_of(i, own)
        z_half = lo if own else other_lo
        part = 0 if own else 1

        @pl.loop(1, PLANE)
        def _(k):
            to = plane_peer(k)
            remote(
                source.at[pl.ds(to * YS, YS)], z_in.at[i, :, plane, z_half],
                zi_s.at[i, part], zi_r.at[i], (row, to * 2 + lo),
            ).start()

        pltpu.make_async_copy(
            source.at[pl.ds(plane * YS, YS)], z_in.at[i, :, plane, z_half], zi_r.at[i]
        ).start()

    def y_target(i, z_half, own, source_row):
        held = y_last if i == LAST and own else y_in.at[i, z_half]
        return held.at[:, source_row]

    def z_target(i, half, own):
        return z_last if i == LAST and own else z_out.at[i, half]

    def send_y(i, own):
        part, z_half = (0, lo) if own else (1, other_lo)
        if not own:
            drain(staged.at[i, pl.ds(0, HALF)], g_l.at[i, 0])
            for n in range(3):
                drain(staged.at[i, pl.ds(0, HALF)], g_s.at[i, 0, n])
        if own and i == 0:
            first_block.wait()
        else:
            fetch(part_of(i, own), block)

        @pl.loop(0, ROWS // 16)
        def _(j):
            turn[pl.ds(j * 16 * ZS, 16 * ZS)] = block[pl.ds(j * 16, 16)].astype(F32).reshape(16 * ZS, LANES)

        @pl.loop(0, ZS)
        def _(z):
            staged[i, z] = turn[pl.ds(z, ROWS, stride=ZS)].astype(BF16)

        keep, give = core * HALF, (1 - core) * HALF
        whole = pl.ds(0, HALF)
        near = y_target(i, z_half, own, row)
        far = y_target(i, z_half, not own, row)
        pieces = [(keep, far_same, 0, far), (give, far_cross, 1, far), (give, sibling, 2, near)]
        if i == LAST and not own:
            for h in range(2):
                for z, peer, n, target in pieces[:2]:
                    remote(
                        staged.at[i, pl.ds(z + h * QUARTER, QUARTER)], target.at[pl.ds(h * QUARTER, QUARTER)],
                        g_s.at[i, part, n], last_r.at[h], peer,
                    ).start()
            pieces = pieces[2:]
        for z, peer, n, target in pieces:
            remote(
                staged.at[i, pl.ds(z, HALF)], target.at[whole], g_s.at[i, part, n], g_r.at[i, z_half], peer
            ).start()
        pltpu.make_async_copy(staged.at[i, pl.ds(keep, HALF)], near.at[whole], g_l.at[i, part]).start()

    def do_z(i):
        drain(z_in.at[i], zi_r.at[i])
        fetch(z_in.at[i], z_pencil)

        @pl.loop(0, YS // 2)
        def _(j):
            def points(y):
                return z_pencil[y].astype(F32).reshape(NZ, LANES).astype(BF16)

            pair = jnp.concatenate([points(2 * j), points(2 * j + 1)], axis=1)
            product = jnp.dot(z_op[...], pair, preferred_element_type=F32)
            for n in range(2):
                result = product[:, n * LANES:(n + 1) * LANES].reshape(PLANE, 2, ZS, LANES)
                z_result[i, 2 * j + n] = result.astype(BF16)

    def return_z(i, own):
        half = lo if own else other_lo
        target = z_target(i, half, own).at[pl.ds(plane * YS, YS)]

        @pl.loop(1, PLANE)
        def _(k):
            to = plane_peer(k)
            remote(
                z_result.at[i, :, to, half], target,
                zo_s.at[i, half], zo_r.at[i, half], (row, to * 2 + lo),
            ).start()

        pltpu.make_async_copy(
            z_result.at[i, :, plane, half], target, zo_r.at[i, half]
        ).start()

    def make_y_op():
        loads[1].wait()
        loads[2].wait()
        for n in range(3):
            here = slice(n * LANES, (n + 1) * LANES)
            there = pl.ds(pl.multiple_of(hi * (2 * ROWS) + n * LANES, LANES), LANES)
            combined = (
                y_stretch[there].reshape(1, LANES) * y_parts[0, :, here].astype(F32)
                + y_curve[there].reshape(1, LANES) * y_parts[1, :, here].astype(F32)
            )
            y_op[here] = combined.T.astype(BF16)

    def make_z_op():
        loads[3].wait()
        for n in range(NZ // LANES):
            here = slice(n * LANES, (n + 1) * LANES)
            z_op[here] = z_raw[:, here].astype(F32).T.astype(BF16)

    def x_store(j, slot):
        return pltpu.make_async_copy(x_result.at[slot], x_term.at[:, pl.ds(j * XS, XS)], x_s.at[slot])

    def do_x(first, last):
        @pl.loop(first, last)
        def _(j):
            slot = lax.rem(j, 2)
            x_load(j, slot).wait()

            @pl.when(j + 1 < ROWS // XS)
            def _():
                x_load(j + 1, 1 - slot).start()

            @pl.when(j >= 2)
            def _():
                x_store(j - 2, slot).wait()

            flat = x_tile[slot].reshape(XS * ZS, 2 * CHUNKS * LANES)
            product = jnp.dot(flat, x_op[...], preferred_element_type=F32)
            for n in range(2 * CHUNKS):
                x_result[slot, n] = product[:, n * LANES:(n + 1) * LANES].reshape(XS, ZS, LANES)
            x_store(j, slot).start()

    def y_products(i, held, first, last):
        @pl.loop(first, last)
        def _(j):
            pair = jnp.concatenate([held[2 * j].reshape(NY, LANES), held[2 * j + 1].reshape(NY, LANES)], axis=1)
            product = jnp.dot(y_op[...], pair, preferred_element_type=F32).astype(BF16)
            for n in range(2):
                for c in range(2):
                    y_result[i, c, 2 * j + n] = product[c * ROWS:(c + 1) * ROWS, n * LANES:(n + 1) * LANES]

    def do_y(i, own):
        part, half = (0, lo) if own else (1, other_lo)
        drain(y_in.at[i, half, :, pl.ds(0, 3)], g_r.at[i, half])
        if own:
            drain(y_got.at[i, 1], ys_s.at[i, 1])
        else:
            drain(staged.at[i, pl.ds(0, HALF)], g_l.at[i, 1])
        fetch(y_in.at[i, half], y_pencil)
        y_products(i, y_pencil, 0, HALF // 2)
        remote(
            y_result.at[i, 1 - core], y_got.at[i, part], ys_s.at[i, part], ys_r.at[i, part], sibling
        ).start()

    def do_y_last(h):
        if h == 0:
            drain(y_got.at[LAST, 1], ys_s.at[LAST, 1])
            drain(y_last.at[:, 0], g_r.at[LAST, lo])
        drain(y_last.at[pl.ds(0, QUARTER), pl.ds(0, 2)], last_r.at[h])
        y_products(LAST, y_last, h * (QUARTER // 2), (h + 1) * (QUARTER // 2))
        piece = pl.ds(h * QUARTER, QUARTER)
        remote(
            y_result.at[LAST, 1 - core, piece], y_got.at[LAST, 0, piece], last_ys_s.at[h], last_ys_r.at[h], sibling
        ).start()

    def x_fetch(i, own):
        return pltpu.make_async_copy(x_term.at[(upper if own else 1 - upper) * CHUNKS + i], x_got, x_g)

    order = [(0, False), (1, False), (0, True), (2, False), (1, True), (2, True), (3, False), (3, True)]

    def keep_rows(i, own, first):
        n, rows = order.index((i, own)) % 2, pl.ds(first, ROWS // 2)
        return pltpu.make_async_copy(
            final.at[n, rows], total.at[rows, :, lanes(mine if own else theirs, i)], keep_l.at[n]
        )

    def slot_for(i, own):
        n = order.index((i, own))
        if n >= 2:
            drain(final.at[n % 2], keep_l.at[n % 2])
        return n % 2

    def combine(i, own):
        part, half = (0, lo) if own else (1, other_lo)
        last = own and i == LAST
        if own:
            x_fetch(i, True).start()

        @pl.loop(0, HALF)
        def _(z):
            turn[pl.ds(core * HALF + z, ROWS, stride=ZS)] = y_result[i, core, z].astype(F32)

        if last:
            z_term = z_last
            for h in range(2):
                drain(y_got.at[i, 0, pl.ds(0, QUARTER)], last_ys_r.at[h])
        else:
            z_term = z_got
            drain(z_out.at[i, half], zo_r.at[i, half])
            z_fetch = pltpu.make_async_copy(z_out.at[i, half], z_got, z_l)
            z_fetch.start()
            drain(y_got.at[i, part], ys_r.at[i, part])

        @pl.loop(0, HALF)
        def _(z):
            turn[pl.ds((1 - core) * HALF + z, ROWS, stride=ZS)] = y_got[i, part, z].astype(F32)

        if own:
            x_fetch(i, True).wait()
            slot = slot_for(i, True)
        if last:
            drain(z_last, zo_r.at[i, half])
        else:
            z_fetch.wait()
        for first in (0, ROWS // 2):
            @pl.loop(0, ROWS // 32)
            def _(j):
                rows = pl.ds(first + j * 16, 16)
                both = turn[pl.ds((first + j * 16) * ZS, 16 * ZS)].reshape(16, ZS, LANES) + z_term[rows].astype(F32)
                if own:
                    final[slot, rows] = (both + x_got[rows]).astype(BF16)
                else:
                    summed[i, rows] = both.astype(BF16)

            if own:
                keep_rows(i, True, first).start()

        if not own:
            remote(summed.at[i], back.at[i], back_s.at[i], back_r.at[i], lo_peer).start()

    def finish(i):
        x_fetch(i, False).start()
        drain(back.at[i], back_r.at[i])
        x_fetch(i, False).wait()
        slot = slot_for(i, False)
        for first in (0, ROWS // 2):
            @pl.loop(0, ROWS // 32)
            def _(j):
                rows = pl.ds(first + j * 16, 16)
                final[slot, rows] = (back[i, rows].astype(F32) + x_got[rows]).astype(BF16)

            keep_rows(i, False, first).start()

    def take(i):
        drain(traded.at[i], lo_r.at[i])
        send_z(i, False)
        send_y(i, False)

    for i in range(CHUNKS):
        remote(field.at[:, :, lanes(theirs, i)], traded.at[i], lo_s.at[i], lo_r.at[i], lo_peer).start()
    send_z(0, True)
    send_y(0, True)
    send_z(1, True)
    send_z(2, True)
    for i in range(1, CHUNKS):
        send_y(i, True)
    loads[0].wait()
    steps = ROWS // XS
    do_x(0, steps // 2)
    take(0)
    make_y_op()
    make_z_op()
    do_y(0, False)
    do_x(steps // 2, steps)
    for slot in range(2):
        x_store(slot, slot).wait()
    take(1)
    do_z(0)
    return_z(0, False)
    send_z(3, True)
    do_y(1, False)
    take(2)
    do_z(1)
    return_z(1, False)
    combine(0, False)
    do_y(2, False)
    take(3)
    do_z(2)
    return_z(2, False)
    combine(1, False)
    do_z(3)
    return_z(3, False)
    for i in range(CHUNKS):
        return_z(i, True)
    do_y(3, False)
    finish(0)
    do_y(0, True)
    combine(2, False)
    combine(3, False)
    finish(1)
    do_y(1, True)
    combine(0, True)
    finish(2)
    do_y(2, True)
    combine(1, True)
    do_y_last(0)
    combine(2, True)
    do_y_last(1)
    finish(3)
    combine(3, True)

    for i in range(CHUNKS):
        drain(traded.at[i], lo_s.at[i])
        for part in range(2):
            drain(z_in.at[i, :, pl.ds(0, PLANE - 1), 0], zi_s.at[i, part])
        for n in range(3):
            drain(staged.at[i, pl.ds(0, HALF)], g_s.at[i, 1, n])
        for half in range(2):
            drain(z_out.at[i, half, pl.ds(0, (PLANE - 1) * YS)], zo_s.at[i, half])
        if i != LAST:
            drain(y_got.at[i, 0], ys_s.at[i, 0])
        drain(summed.at[i], back_s.at[i])
    for n in range(2):
        drain(final.at[n], keep_l.at[n])
        drain(y_got.at[LAST, 0, pl.ds(0, QUARTER)], last_ys_s.at[n])


def laplacian(*operands):
    any_space, vmem = pl.BlockSpec(memory_space=pl.ANY), pl.BlockSpec(memory_space=pltpu.VMEM)
    shape = lambda *dims: jax.ShapeDtypeStruct(dims, BF16)
    held = lambda *dims: pltpu.VMEM(dims, BF16)
    dma = pltpu.SemaphoreType.DMA
    nx = 2 * CHUNKS * LANES
    return pl.pallas_call(
        laplacian_kernel,
        name="laplacian",
        out_shape=(
            shape(ROWS, ZS, nx),
            shape(CHUNKS, ROWS, ZS, LANES),
            shape(CHUNKS, YS, PLANE, 2, ZS, LANES),
            shape(CHUNKS, 2, HALF, 4, ROWS, LANES),
            shape(CHUNKS, 2, ROWS, ZS, LANES),
            jax.ShapeDtypeStruct((2 * CHUNKS, ROWS, ZS, LANES), F32),
        ),
        in_specs=[any_space] * 4 + [vmem] * 2 + [any_space],
        out_specs=(any_space,) * 6,
        scratch_shapes=[
            held(nx, nx), held(2, NY, 2 * ROWS), held(2 * ROWS, NY), held(NZ, NZ), held(NZ, NZ),
            held(2, XS, ZS, nx),
            pltpu.VMEM((2, 2 * CHUNKS, XS, ZS, LANES), F32),
            pltpu.VMEM((ROWS, ZS, LANES), F32),
            pltpu.VMEM((ROWS * ZS, LANES), F32),
            held(CHUNKS, ZS, ROWS, LANES),
            held(ROWS, ZS, LANES),
            held(YS, PLANE, 2, ZS, LANES),
            held(CHUNKS, YS, PLANE, 2, ZS, LANES),
            held(HALF, 4, ROWS, LANES),
            held(CHUNKS, 2, HALF, ROWS, LANES),
            held(CHUNKS, 2, HALF, ROWS, LANES),
            held(ROWS, ZS, LANES),
            held(CHUNKS, ROWS, ZS, LANES),
            held(2, ROWS, ZS, LANES),
            held(CHUNKS, ROWS, ZS, LANES), held(HALF, 4, ROWS, LANES), held(ROWS, ZS, LANES),
            dma((CHUNKS,)), dma((CHUNKS,)),
            dma((CHUNKS, 2)), dma((CHUNKS,)),
            dma((CHUNKS, 2, 3)), dma((CHUNKS, 2)), dma((CHUNKS, 2)),
            dma((CHUNKS, 2)), dma((CHUNKS, 2)),
            dma((CHUNKS, 2)), dma((CHUNKS, 2)),
            dma((CHUNKS,)), dma((CHUNKS,)),
            dma((2,)), dma, dma((4,)), dma((2,)), dma((2,)), dma,
            dma, dma((2,)), dma((2,)), dma((2,)),
        ],
        compiler_params=pltpu.CompilerParams(
            collective_id=0, has_side_effects=True, vmem_limit_bytes=62 * 2**20
        ),
        cost_estimate=pl.CostEstimate(flops=24_200_000_000, bytes_accessed=180_000_000, transcendentals=0),
    )(*operands)[0]


def copy_kernel(source, target, held, read, written):
    parts = read.shape[0]
    rows = source.shape[0] // parts
    piece = lambda n: pl.ds(n * rows, rows)
    reads = [pltpu.make_async_copy(source.at[piece(n)], held.at[piece(n)], read.at[n]) for n in range(parts)]
    writes = [pltpu.make_async_copy(held.at[piece(n)], target.at[piece(n)], written.at[n]) for n in range(parts)]
    for copy in reads:
        copy.start()
    for n in range(parts):
        reads[n].wait()
        writes[n].start()
    for copy in writes:
        copy.wait()


def copied(array):
    any_space = pl.BlockSpec(memory_space=pl.ANY)
    parts = 12
    return pl.pallas_call(
        copy_kernel,
        name="result",
        in_specs=[any_space],
        out_specs=any_space,
        out_shape=jax.ShapeDtypeStruct(array.shape, array.dtype),
        scratch_shapes=[
            pltpu.VMEM(array.shape, array.dtype),
            pltpu.SemaphoreType.DMA((parts,)), pltpu.SemaphoreType.DMA((parts,)),
        ],
        compiler_params=pltpu.CompilerParams(vmem_limit_bytes=60 * 2**20),
    )(array)


def per_device(scalar_field, x_operator, y_second, y_first, y_stretch, y_curve, z_operator):
    return copied(laplacian(
        scalar_field, x_operator, y_second, y_first, y_stretch, y_curve, z_operator
    ))


def solution(mesh):
    in_specs = (P("row", "col", None), P(), P(), P(), P(), P(), P())
    out_specs = P("row", "col", None)
    return jax.shard_map(
        per_device, mesh=mesh, in_specs=in_specs, out_specs=out_specs, check_vma=False
    )
```

```python
import jax
import jax.numpy as jnp
from jax import lax
from jax.experimental import pallas as pl
from jax.experimental.pallas import tpu as pltpu
from jax.sharding import PartitionSpec as P

MESH = pl.DeviceIdType.MESH
BF16 = jnp.bfloat16
F32 = jnp.float32
LANES = 128
CHUNKS = 4
PLANE = 16
ROWS = 192
ZS = 24
YS = ROWS // PLANE
HALF = ZS // 2
QUARTER = HALF // 2
LAST = CHUNKS - 1
XS = 8
NY = 4 * ROWS
NZ = 2 * PLANE * ZS


def laplacian_kernel(
    field, x_source, y_second, y_first, y_stretch, y_curve, z_source,
    total, traded, z_in, y_in, z_out, x_term,
    x_op, y_parts, y_op, z_raw, z_op, x_tile, x_result, x_got,
    turn, staged, block, z_pencil, z_result, y_pencil, y_result, y_got, z_got, summed,
    back, y_last, z_last,
    lo_s, lo_r, zi_s, zi_r, g_s, g_l, g_r, zo_s, zo_r, ys_s, ys_r, back_s, back_r, load, ops_l, x_l, x_s,
    x_g, z_l, last_r, last_ys_s, last_ys_r,
):
    row, col = lax.axis_index("row"), lax.axis_index("col")
    hi, core = row // 2, row % 2
    plane, lo = col // 2, col % 2
    pz, py = plane // 4, plane % 4
    upper = 1 - lax.rem(hi + lo, 2)
    mine, theirs = upper * (CHUNKS * LANES), (1 - upper) * (CHUNKS * LANES)
    other_lo = 1 - lo

    lo_peer = (row, plane * 2 + other_lo)
    sibling = (hi * 2 + 1 - core, col)
    far_same = ((1 - hi) * 2 + core, plane * 2 + other_lo)
    far_cross = ((1 - hi) * 2 + 1 - core, plane * 2 + other_lo)

    def plane_peer(k):
        k = lax.rem(k * 7, PLANE)
        return lax.rem(pz + k // 4, 4) * 4 + lax.rem(py + k % 4, 4)

    def lanes(start, i):
        return pl.ds(pl.multiple_of(start + i * LANES, LANES), LANES)

    def remote(src, dst, send, recv, device):
        return pltpu.make_async_remote_copy(
            src_ref=src, dst_ref=dst, send_sem=send, recv_sem=recv, device_id=device, device_id_type=MESH
        )

    def drain(ref, sem):
        pltpu.make_async_copy(ref, ref, sem).wait()

    def fetch(src, dst):
        copy = pltpu.make_async_copy(src, dst, load)
        copy.start()
        copy.wait()

    y_columns = pl.ds(pl.multiple_of(hi * (2 * ROWS), LANES), 2 * ROWS)
    loads = [
        pltpu.make_async_copy(source, target, ops_l.at[n])
        for n, (source, target) in enumerate((
            (x_source, x_op), (y_second.at[:, y_columns], y_parts.at[0]),
            (y_first.at[:, y_columns], y_parts.at[1]), (z_source, z_raw),
        ))
    ]
    for copy in loads:
        copy.start()

    def x_load(j, slot):
        return pltpu.make_async_copy(field.at[pl.ds(j * XS, XS)], x_tile.at[slot], x_l.at[slot])

    barrier = pltpu.get_barrier_semaphore()
    for peer in (lo_peer, sibling, far_same, far_cross):
        pl.semaphore_signal(barrier, inc=1, device_id=peer, device_id_type=MESH)

    @pl.loop(1, PLANE)
    def _(k):
        pl.semaphore_signal(barrier, inc=1, device_id=(row, plane_peer(k) * 2 + lo), device_id_type=MESH)

    first_block = pltpu.make_async_copy(field.at[:, :, lanes(mine, 0)], block, load)
    first_block.start()
    x_load(0, 0).start()
    pl.semaphore_wait(barrier, 4 + PLANE - 1)

    def part_of(i, own):
        return field.at[:, :, lanes(mine, i)] if own else traded.at[i]

    def send_z(i, own):
        source = part_of(i, own)
        z_half = lo if own else other_lo
        part = 0 if own else 1

        @pl.loop(1, PLANE)
        def _(k):
            to = plane_peer(k)
            remote(
                source.at[pl.ds(to * YS, YS)], z_in.at[i, :, plane, z_half],
                zi_s.at[i, part], zi_r.at[i], (row, to * 2 + lo),
            ).start()

        pltpu.make_async_copy(
            source.at[pl.ds(plane * YS, YS)], z_in.at[i, :, plane, z_half], zi_r.at[i]
        ).start()

    def y_target(i, z_half, own, source_row):
        held = y_last if i == LAST and own else y_in.at[i, z_half]
        return held.at[:, source_row]

    def z_target(i, half, own):
        return z_last if i == LAST and own else z_out.at[i, half]

    def send_y(i, own):
        part, z_half = (0, lo) if own else (1, other_lo)
        if not own:
            drain(staged.at[i, pl.ds(0, HALF)], g_l.at[i, 0])
            for n in range(3):
                drain(staged.at[i, pl.ds(0, HALF)], g_s.at[i, 0, n])
        if own and i == 0:
            first_block.wait()
        else:
            fetch(part_of(i, own), block)

        @pl.loop(0, ROWS // 16)
        def _(j):
            turn[pl.ds(j * 16 * ZS, 16 * ZS)] = block[pl.ds(j * 16, 16)].astype(F32).reshape(16 * ZS, LANES)

        @pl.loop(0, ZS)
        def _(z):
            staged[i, z] = turn[pl.ds(z, ROWS, stride=ZS)].astype(BF16)

        keep, give = core * HALF, (1 - core) * HALF
        whole = pl.ds(0, HALF)
        near = y_target(i, z_half, own, row)
        far = y_target(i, z_half, not own, row)
        pieces = [(keep, far_same, 0, far), (give, far_cross, 1, far), (give, sibling, 2, near)]
        if i == LAST and not own:
            for h in range(2):
                for z, peer, n, target in pieces[:2]:
                    remote(
                        staged.at[i, pl.ds(z + h * QUARTER, QUARTER)], target.at[pl.ds(h * QUARTER, QUARTER)],
                        g_s.at[i, part, n], last_r.at[h], peer,
                    ).start()
            pieces = pieces[2:]
        for z, peer, n, target in pieces:
            remote(
                staged.at[i, pl.ds(z, HALF)], target.at[whole], g_s.at[i, part, n], g_r.at[i, z_half], peer
            ).start()
        pltpu.make_async_copy(staged.at[i, pl.ds(keep, HALF)], near.at[whole], g_l.at[i, part]).start()

    def do_z(i):
        drain(z_in.at[i], zi_r.at[i])
        fetch(z_in.at[i], z_pencil)

        @pl.loop(0, YS // 2)
        def _(j):
            def points(y):
                return z_pencil[y].astype(F32).reshape(NZ, LANES).astype(BF16)

            pair = jnp.concatenate([points(2 * j), points(2 * j + 1)], axis=1)
            product = jnp.dot(z_op[...], pair, preferred_element_type=F32)
            for n in range(2):
                result = product[:, n * LANES:(n + 1) * LANES].reshape(PLANE, 2, ZS, LANES)
                z_result[i, 2 * j + n] = result.astype(BF16)

    def return_z(i, own):
        half = lo if own else other_lo
        target = z_target(i, half, own).at[pl.ds(plane * YS, YS)]

        @pl.loop(1, PLANE)
        def _(k):
            to = plane_peer(k)
            remote(
                z_result.at[i, :, to, half], target,
                zo_s.at[i, half], zo_r.at[i, half], (row, to * 2 + lo),
            ).start()

        pltpu.make_async_copy(
            z_result.at[i, :, plane, half], target, zo_r.at[i, half]
        ).start()

    def make_y_op():
        loads[1].wait()
        loads[2].wait()
        for n in range(3):
            here = slice(n * LANES, (n + 1) * LANES)
            there = pl.ds(pl.multiple_of(hi * (2 * ROWS) + n * LANES, LANES), LANES)
            combined = (
                y_stretch[there].reshape(1, LANES) * y_parts[0, :, here].astype(F32)
                + y_curve[there].reshape(1, LANES) * y_parts[1, :, here].astype(F32)
            )
            y_op[here] = combined.T.astype(BF16)

    def make_z_op():
        loads[3].wait()
        for n in range(NZ // LANES):
            here = slice(n * LANES, (n + 1) * LANES)
            z_op[here] = z_raw[:, here].astype(F32).T.astype(BF16)

    def x_store(j, slot):
        return pltpu.make_async_copy(x_result.at[slot], x_term.at[:, pl.ds(j * XS, XS)], x_s.at[slot])

    def do_x(first, last):
        @pl.loop(first, last)
        def _(j):
            slot = lax.rem(j, 2)
            x_load(j, slot).wait()

            @pl.when(j + 1 < ROWS // XS)
            def _():
                x_load(j + 1, 1 - slot).start()

            @pl.when(j >= 2)
            def _():
                x_store(j - 2, slot).wait()

            flat = x_tile[slot].reshape(XS * ZS, 2 * CHUNKS * LANES)
            product = jnp.dot(flat, x_op[...], preferred_element_type=F32)
            for n in range(2 * CHUNKS):
                x_result[slot, n] = product[:, n * LANES:(n + 1) * LANES].reshape(XS, ZS, LANES)
            x_store(j, slot).start()

    def y_products(i, held, first, last):
        @pl.loop(first, last)
        def _(j):
            pair = jnp.concatenate([held[2 * j].reshape(NY, LANES), held[2 * j + 1].reshape(NY, LANES)], axis=1)
            product = jnp.dot(y_op[...], pair, preferred_element_type=F32).astype(BF16)
            for n in range(2):
                for c in range(2):
                    y_result[i, c, 2 * j + n] = product[c * ROWS:(c + 1) * ROWS, n * LANES:(n + 1) * LANES]

    def do_y(i, own):
        part, half = (0, lo) if own else (1, other_lo)
        drain(y_in.at[i, half, :, pl.ds(0, 3)], g_r.at[i, half])
        if own:
            drain(y_got.at[i, 1], ys_s.at[i, 1])
        else:
            drain(staged.at[i, pl.ds(0, HALF)], g_l.at[i, 1])
        fetch(y_in.at[i, half], y_pencil)
        y_products(i, y_pencil, 0, HALF // 2)
        remote(
            y_result.at[i, 1 - core], y_got.at[i, part], ys_s.at[i, part], ys_r.at[i, part], sibling
        ).start()

    def do_y_last(h):
        if h == 0:
            drain(y_got.at[LAST, 1], ys_s.at[LAST, 1])
            drain(y_last.at[:, 0], g_r.at[LAST, lo])
        drain(y_last.at[pl.ds(0, QUARTER), pl.ds(0, 2)], last_r.at[h])
        y_products(LAST, y_last, h * (QUARTER // 2), (h + 1) * (QUARTER // 2))
        piece = pl.ds(h * QUARTER, QUARTER)
        remote(
            y_result.at[LAST, 1 - core, piece], y_got.at[LAST, 0, piece], last_ys_s.at[h], last_ys_r.at[h], sibling
        ).start()

    def x_fetch(i, own):
        return pltpu.make_async_copy(x_term.at[(upper if own else 1 - upper) * CHUNKS + i], x_got, x_g)

    def combine(i, own):
        part, half = (0, lo) if own else (1, other_lo)
        last = own and i == LAST
        if own:
            x_fetch(i, True).start()

        @pl.loop(0, HALF)
        def _(z):
            turn[pl.ds(core * HALF + z, ROWS, stride=ZS)] = y_result[i, core, z].astype(F32)

        if last:
            z_term = z_last
            for h in range(2):
                drain(y_got.at[i, 0, pl.ds(0, QUARTER)], last_ys_r.at[h])
        else:
            z_term = z_got
            drain(z_out.at[i, half], zo_r.at[i, half])
            z_fetch = pltpu.make_async_copy(z_out.at[i, half], z_got, z_l)
            z_fetch.start()
            drain(y_got.at[i, part], ys_r.at[i, part])

        @pl.loop(0, HALF)
        def _(z):
            turn[pl.ds((1 - core) * HALF + z, ROWS, stride=ZS)] = y_got[i, part, z].astype(F32)

        if own:
            x_fetch(i, True).wait()
        elif i >= 2:
            drain(summed.at[i % 2], back_s.at[i - 2])
        if last:
            drain(z_last, zo_r.at[i, half])
        else:
            z_fetch.wait()
        @pl.loop(0, ROWS // 16)
        def _(j):
            rows = pl.ds(j * 16, 16)
            both = turn[pl.ds(j * 16 * ZS, 16 * ZS)].reshape(16, ZS, LANES) + z_term[rows].astype(F32)
            if own:
                total[rows, :, lanes(mine, i)] = (both + x_got[rows]).astype(BF16)
            else:
                summed[i % 2, rows] = both.astype(BF16)

        if not own:
            remote(summed.at[i % 2], back.at[i], back_s.at[i], back_r.at[i], lo_peer).start()

    def finish(i):
        x_fetch(i, False).start()
        drain(back.at[i], back_r.at[i])
        x_fetch(i, False).wait()

        @pl.loop(0, ROWS // 16)
        def _(j):
            rows = pl.ds(j * 16, 16)
            total[rows, :, lanes(theirs, i)] = (back[i, rows].astype(F32) + x_got[rows]).astype(BF16)

    def take(i):
        drain(traded.at[i], lo_r.at[i])
        send_z(i, False)
        send_y(i, False)

    for i in range(CHUNKS):
        remote(field.at[:, :, lanes(theirs, i)], traded.at[i], lo_s.at[i], lo_r.at[i], lo_peer).start()
    send_z(0, True)
    send_y(0, True)
    send_z(1, True)
    send_z(2, True)
    for i in range(1, CHUNKS):
        send_y(i, True)
    loads[0].wait()
    do_x(0, 8)
    take(0)
    make_y_op()
    make_z_op()
    do_y(0, False)
    do_x(8, 13)
    take(1)
    do_z(0)
    return_z(0, False)
    send_z(3, True)
    do_y(1, False)
    do_x(13, 18)
    take(2)
    do_z(1)
    return_z(1, False)
    combine(0, False)
    do_y(2, False)
    do_x(18, 21)
    take(3)
    do_z(2)
    return_z(2, False)
    combine(1, False)
    do_x(21, 24)
    do_z(3)
    return_z(3, False)
    for i in range(CHUNKS):
        return_z(i, True)
    for slot in range(2):
        x_store(slot, slot).wait()
    do_y(3, False)
    finish(0)
    do_y(0, True)
    combine(2, False)
    combine(3, False)
    finish(1)
    do_y(1, True)
    combine(0, True)
    finish(2)
    do_y(2, True)
    combine(1, True)
    do_y_last(0)
    combine(2, True)
    do_y_last(1)
    finish(3)
    combine(3, True)

    for i in range(CHUNKS):
        drain(traded.at[i], lo_s.at[i])
        for part in range(2):
            drain(z_in.at[i, :, pl.ds(0, PLANE - 1), 0], zi_s.at[i, part])
        for n in range(3):
            drain(staged.at[i, pl.ds(0, HALF)], g_s.at[i, 1, n])
        for half in range(2):
            drain(z_out.at[i, half, pl.ds(0, (PLANE - 1) * YS)], zo_s.at[i, half])
        if i != LAST:
            drain(y_got.at[i, 0], ys_s.at[i, 0])
        if i >= 2:
            drain(summed.at[i % 2], back_s.at[i])
    for n in range(2):
        drain(y_got.at[LAST, 0, pl.ds(0, QUARTER)], last_ys_s.at[n])


def laplacian(*operands):
    any_space, vmem = pl.BlockSpec(memory_space=pl.ANY), pl.BlockSpec(memory_space=pltpu.VMEM)
    shape = lambda *dims: jax.ShapeDtypeStruct(dims, BF16)
    held = lambda *dims: pltpu.VMEM(dims, BF16)
    dma = pltpu.SemaphoreType.DMA
    nx = 2 * CHUNKS * LANES
    return pl.pallas_call(
        laplacian_kernel,
        name="laplacian",
        out_shape=(
            held(ROWS, ZS, nx),
            shape(CHUNKS, ROWS, ZS, LANES),
            shape(CHUNKS, YS, PLANE, 2, ZS, LANES),
            shape(CHUNKS, 2, HALF, 4, ROWS, LANES),
            shape(CHUNKS, 2, ROWS, ZS, LANES),
            jax.ShapeDtypeStruct((2 * CHUNKS, ROWS, ZS, LANES), F32),
        ),
        in_specs=[any_space] * 4 + [vmem] * 2 + [any_space],
        out_specs=(vmem,) + (any_space,) * 5,
        scratch_shapes=[
            held(nx, nx), held(2, NY, 2 * ROWS), held(2 * ROWS, NY), held(NZ, NZ), held(NZ, NZ),
            held(2, XS, ZS, nx),
            pltpu.VMEM((2, 2 * CHUNKS, XS, ZS, LANES), F32),
            pltpu.VMEM((ROWS, ZS, LANES), F32),
            pltpu.VMEM((ROWS * ZS, LANES), F32),
            held(CHUNKS, ZS, ROWS, LANES),
            held(ROWS, ZS, LANES),
            held(YS, PLANE, 2, ZS, LANES),
            held(CHUNKS, YS, PLANE, 2, ZS, LANES),
            held(HALF, 4, ROWS, LANES),
            held(CHUNKS, 2, HALF, ROWS, LANES),
            held(CHUNKS, 2, HALF, ROWS, LANES),
            held(ROWS, ZS, LANES),
            held(2, ROWS, ZS, LANES),
            held(CHUNKS, ROWS, ZS, LANES), held(HALF, 4, ROWS, LANES), held(ROWS, ZS, LANES),
            dma((CHUNKS,)), dma((CHUNKS,)),
            dma((CHUNKS, 2)), dma((CHUNKS,)),
            dma((CHUNKS, 2, 3)), dma((CHUNKS, 2)), dma((CHUNKS, 2)),
            dma((CHUNKS, 2)), dma((CHUNKS, 2)),
            dma((CHUNKS, 2)), dma((CHUNKS, 2)),
            dma((CHUNKS,)), dma((CHUNKS,)),
            dma, dma((4,)), dma((2,)), dma((2,)), dma,
            dma, dma((2,)), dma((2,)), dma((2,)),
        ],
        compiler_params=pltpu.CompilerParams(
            collective_id=0, has_side_effects=True, vmem_limit_bytes=54 * 2**20
        ),
        cost_estimate=pl.CostEstimate(flops=24_200_000_000, bytes_accessed=180_000_000, transcendentals=0),
    )(*operands)[0]


def write_kernel(source, target, sems):
    parts = sems.shape[0]
    rows = source.shape[0] // parts
    copies = [
        pltpu.make_async_copy(source.at[pl.ds(n * rows, rows)], target.at[pl.ds(n * rows, rows)], sems.at[n])
        for n in range(parts)
    ]
    for copy in copies:
        copy.start()
    for copy in copies:
        copy.wait()


def written(array):
    return pl.pallas_call(
        write_kernel,
        name="result",
        in_specs=[pl.BlockSpec(memory_space=pltpu.VMEM)],
        out_specs=pl.BlockSpec(memory_space=pl.ANY),
        out_shape=jax.ShapeDtypeStruct(array.shape, array.dtype),
        scratch_shapes=[pltpu.SemaphoreType.DMA((4,))],
        compiler_params=pltpu.CompilerParams(vmem_limit_bytes=16 * 2**20),
    )(array)


def per_device(scalar_field, x_operator, y_second, y_first, y_stretch, y_curve, z_operator):
    return written(laplacian(
        scalar_field, x_operator, y_second, y_first, y_stretch, y_curve, z_operator
    ))


def solution(mesh):
    in_specs = (P("row", "col", None), P(), P(), P(), P(), P(), P())
    out_specs = P("row", "col", None)
    return jax.shard_map(
        per_device, mesh=mesh, in_specs=in_specs, out_specs=out_specs, check_vma=False
    )
```

```python
import jax
import jax.numpy as jnp
from jax import lax
from jax.experimental import pallas as pl
from jax.experimental.pallas import tpu as pltpu
from jax.sharding import PartitionSpec as P

MESH = pl.DeviceIdType.MESH
BF16 = jnp.bfloat16
F32 = jnp.float32
LANES = 128
CHUNKS = 4
PLANE = 16
ROWS = 192
ZS = 24
YS = ROWS // PLANE
HALF = ZS // 2
QUARTER = HALF // 2
LAST = CHUNKS - 1
XS = 8
NY = 4 * ROWS
NZ = 2 * PLANE * ZS


def laplacian_kernel(
    field, x_source, y_second, y_first, y_stretch, y_curve, z_source,
    total, traded, z_in, y_in, z_out, x_term,
    x_op, y_parts, y_op, z_raw, z_op, x_tile, x_result, x_got,
    turn, staged, block, z_pencil, z_result, y_pencil, y_result, y_got, z_got, summed,
    back, y_last, z_last,
    lo_s, lo_r, zi_s, zi_r, g_s, g_l, g_r, zo_s, zo_r, ys_s, ys_r, back_s, back_r, load, ops_l, x_l, x_s,
    x_g, z_l, last_r, last_ys_s, last_ys_r,
):
    row, col = lax.axis_index("row"), lax.axis_index("col")
    hi, core = row // 2, row % 2
    plane, lo = col // 2, col % 2
    pz, py = plane // 4, plane % 4
    upper = 1 - lax.rem(hi + lo, 2)
    mine, theirs = upper * (CHUNKS * LANES), (1 - upper) * (CHUNKS * LANES)
    other_lo, other_core = 1 - lo, 1 - core

    lo_peer = (row, plane * 2 + other_lo)
    sibling = (hi * 2 + 1 - core, col)
    far_same = ((1 - hi) * 2 + core, plane * 2 + other_lo)
    far_cross = ((1 - hi) * 2 + 1 - core, plane * 2 + other_lo)

    def plane_peer(k):
        k = lax.rem(k * 7, PLANE)
        return lax.rem(pz + k // 4, 4) * 4 + lax.rem(py + k % 4, 4)

    def lanes(start, i):
        return pl.ds(pl.multiple_of(start + i * LANES, LANES), LANES)

    def remote(src, dst, send, recv, device):
        return pltpu.make_async_remote_copy(
            src_ref=src, dst_ref=dst, send_sem=send, recv_sem=recv, device_id=device, device_id_type=MESH
        )

    def drain(ref, sem):
        pltpu.make_async_copy(ref, ref, sem).wait()

    def fetch(src, dst):
        copy = pltpu.make_async_copy(src, dst, load)
        copy.start()
        copy.wait()

    y_columns = pl.ds(pl.multiple_of(hi * (2 * ROWS), LANES), 2 * ROWS)
    loads = [
        pltpu.make_async_copy(source, target, ops_l.at[n])
        for n, (source, target) in enumerate((
            (x_source, x_op), (y_second.at[:, y_columns], y_parts.at[0]),
            (y_first.at[:, y_columns], y_parts.at[1]), (z_source, z_raw),
        ))
    ]
    for copy in loads:
        copy.start()

    def x_load(j, slot):
        return pltpu.make_async_copy(field.at[pl.ds(j * XS, XS)], x_tile.at[slot], x_l.at[slot])

    first_block = pltpu.make_async_copy(field.at[:, :, lanes(mine, 0)], block, load)
    first_block.start()
    x_load(0, 0).start()

    barrier = pltpu.get_barrier_semaphore()
    for peer in (lo_peer, sibling, far_same, far_cross):
        pl.semaphore_signal(barrier, inc=1, device_id=peer, device_id_type=MESH)

    @pl.loop(1, PLANE)
    def _(k):
        pl.semaphore_signal(barrier, inc=1, device_id=(row, plane_peer(k) * 2 + lo), device_id_type=MESH)

    def turn_block(i):
        @pl.loop(0, ROWS // 16)
        def _(j):
            turn[pl.ds(j * 16 * ZS, 16 * ZS)] = block[pl.ds(j * 16, 16)].astype(F32).reshape(16 * ZS, LANES)

        @pl.loop(0, ZS)
        def _(z):
            staged[i, z] = turn[pl.ds(z, ROWS, stride=ZS)].astype(BF16)

    first_block.wait()
    turn_block(0)
    pl.semaphore_wait(barrier, 4 + PLANE - 1)

    def part_of(i, own):
        return field.at[:, :, lanes(mine, i)] if own else traded.at[i]

    def send_z(i, own):
        source = part_of(i, own)
        z_half = lo if own else other_lo
        part = 0 if own else 1

        @pl.loop(1, PLANE)
        def _(k):
            to = plane_peer(k)
            remote(
                source.at[pl.ds(to * YS, YS)], z_in.at[i, :, plane, z_half],
                zi_s.at[i, part], zi_r.at[i], (row, to * 2 + lo),
            ).start()

        pltpu.make_async_copy(
            source.at[pl.ds(plane * YS, YS)], z_in.at[i, :, plane, z_half], zi_r.at[i]
        ).start()

    def y_target(i, z_half, own, source_row):
        held = y_last if i == LAST and own else y_in.at[i, z_half]
        return held.at[:, source_row]

    def z_target(i, half, own):
        return z_last if i == LAST and own else z_out.at[i, half]

    def send_y(i, own):
        part, z_half = (0, lo) if own else (1, other_lo)
        if not own:
            drain(staged.at[i, pl.ds(0, HALF)], g_l.at[i, 0])
            for n in range(3):
                drain(staged.at[i, pl.ds(0, HALF)], g_s.at[i, 0, n])
        if not (own and i == 0):
            fetch(part_of(i, own), block)

        if not (own and i == 0):
            turn_block(i)

        keep, give = core * HALF, (1 - core) * HALF
        whole = pl.ds(0, HALF)
        near = y_target(i, z_half, own, row)
        far = y_target(i, z_half, not own, row)
        pieces = [(keep, far_same, 0, far), (give, far_cross, 1, far), (give, sibling, 2, near)]
        if i == LAST and not own:
            for h in range(2):
                for z, peer, n, target in pieces[:2]:
                    remote(
                        staged.at[i, pl.ds(z + h * QUARTER, QUARTER)], target.at[pl.ds(h * QUARTER, QUARTER)],
                        g_s.at[i, part, n], last_r.at[h], peer,
                    ).start()
            pieces = pieces[2:]
        for z, peer, n, target in pieces:
            remote(
                staged.at[i, pl.ds(z, HALF)], target.at[whole], g_s.at[i, part, n], g_r.at[i, z_half], peer
            ).start()
        pltpu.make_async_copy(staged.at[i, pl.ds(keep, HALF)], near.at[whole], g_l.at[i, part]).start()

    def do_z(i):
        drain(z_in.at[i], zi_r.at[i])
        fetch(z_in.at[i], z_pencil)

        @pl.loop(0, YS // 2)
        def _(j):
            def points(y):
                return z_pencil[y].astype(F32).reshape(NZ, LANES).astype(BF16)

            pair = jnp.concatenate([points(2 * j), points(2 * j + 1)], axis=1)
            product = jnp.dot(z_op[...], pair, preferred_element_type=F32)
            for n in range(2):
                result = product[:, n * LANES:(n + 1) * LANES].reshape(PLANE, 2, ZS, LANES)
                z_result[i, 2 * j + n] = result.astype(BF16)

    def return_z(i, own):
        half = lo if own else other_lo
        target = z_target(i, half, own).at[pl.ds(plane * YS, YS)]

        @pl.loop(1, PLANE)
        def _(k):
            to = plane_peer(k)
            remote(
                z_result.at[i, :, to, half], target,
                zo_s.at[i, half], zo_r.at[i, half], (row, to * 2 + lo),
            ).start()

        pltpu.make_async_copy(
            z_result.at[i, :, plane, half], target, zo_r.at[i, half]
        ).start()

    def make_y_op():
        loads[1].wait()
        loads[2].wait()
        for n in range(3):
            here = slice(n * LANES, (n + 1) * LANES)
            there = pl.ds(pl.multiple_of(hi * (2 * ROWS) + n * LANES, LANES), LANES)
            combined = (
                y_stretch[there].reshape(1, LANES) * y_parts[0, :, here].astype(F32)
                + y_curve[there].reshape(1, LANES) * y_parts[1, :, here].astype(F32)
            )
            y_op[here] = combined.T.astype(BF16)

    def make_z_op():
        loads[3].wait()
        for n in range(NZ // LANES):
            here = slice(n * LANES, (n + 1) * LANES)
            z_op[here] = z_raw[:, here].astype(F32).T.astype(BF16)

    def x_store(j, slot):
        return pltpu.make_async_copy(x_result.at[slot], x_term.at[:, pl.ds(j * (XS * ZS), XS * ZS)], x_s.at[slot])

    def do_x(first, last):
        @pl.loop(first, last)
        def _(j):
            slot = lax.rem(j, 2)
            x_load(j, slot).wait()

            @pl.when(j + 1 < ROWS // XS)
            def _():
                x_load(j + 1, 1 - slot).start()

            @pl.when(j >= 2)
            def _():
                x_store(j - 2, slot).wait()

            flat = x_tile[slot].reshape(XS * ZS, 2 * CHUNKS * LANES)
            product = jnp.dot(flat, x_op[...], preferred_element_type=F32)
            for n in range(2 * CHUNKS):
                x_result[slot, n] = product[:, n * LANES:(n + 1) * LANES]
            x_store(j, slot).start()

    def y_products(i, held, first, last):
        @pl.loop(first, last)
        def _(j):
            pair = jnp.concatenate([held[2 * j].reshape(NY, LANES), held[2 * j + 1].reshape(NY, LANES)], axis=1)
            product = jnp.dot(y_op[...], pair, preferred_element_type=F32).astype(BF16)
            for n in range(2):
                for c in range(2):
                    y_result[i, c, 2 * j + n] = product[c * ROWS:(c + 1) * ROWS, n * LANES:(n + 1) * LANES]

    def do_y(i, own):
        part, half = (0, lo) if own else (1, other_lo)
        drain(y_in.at[i, half, :, pl.ds(0, 3)], g_r.at[i, half])
        if own:
            drain(y_got.at[i, 1], ys_s.at[i, 1])
        else:
            drain(staged.at[i, pl.ds(0, HALF)], g_l.at[i, 1])
        fetch(y_in.at[i, half], y_pencil)
        y_products(i, y_pencil, 0, HALF // 2)
        remote(
            y_result.at[i, 1 - core], y_got.at[i, part], ys_s.at[i, part], ys_r.at[i, part], sibling
        ).start()

    def do_y_last(h):
        if h == 0:
            drain(y_got.at[LAST, 1], ys_s.at[LAST, 1])
            drain(y_last.at[:, 0], g_r.at[LAST, lo])
        drain(y_last.at[pl.ds(0, QUARTER), pl.ds(0, 2)], last_r.at[h])
        y_products(LAST, y_last, h * (QUARTER // 2), (h + 1) * (QUARTER // 2))
        piece = pl.ds(h * QUARTER, QUARTER)
        remote(
            y_result.at[LAST, 1 - core, piece], y_got.at[LAST, 0, piece], last_ys_s.at[h], last_ys_r.at[h], sibling
        ).start()

    def x_fetch(i, own):
        return pltpu.make_async_copy(x_term.at[(upper if own else 1 - upper) * CHUNKS + i], x_got, x_g)

    def sixteen(ref, j):
        return ref[pl.ds(j * (16 * ZS), 16 * ZS)].reshape(16, ZS, LANES)

    def combine(i, own):
        part, half = (0, lo) if own else (1, other_lo)
        if own:
            x_fetch(i, True).start()

        @pl.loop(0, HALF)
        def _(z):
            turn[pl.ds(core * HALF + z, ROWS, stride=ZS)] = y_result[i, core, z].astype(F32)

        drain(z_out.at[i, half], zo_r.at[i, half])
        z_fetch = pltpu.make_async_copy(z_out.at[i, half], z_got, z_l)
        z_fetch.start()
        drain(y_got.at[i, part], ys_r.at[i, part])

        @pl.loop(0, HALF)
        def _(z):
            turn[pl.ds((1 - core) * HALF + z, ROWS, stride=ZS)] = y_got[i, part, z].astype(F32)

        if own:
            x_fetch(i, True).wait()
        elif i >= 2:
            drain(summed.at[i % 2], back_s.at[i - 2])
        z_fetch.wait()

        @pl.loop(0, ROWS // 16)
        def _(j):
            rows = pl.ds(j * 16, 16)
            both = sixteen(turn, j) + z_got[rows].astype(F32)
            if own:
                total[rows, :, lanes(mine, i)] = (both + sixteen(x_got, j)).astype(BF16)
            else:
                summed[i % 2, rows] = both.astype(BF16)

        if not own:
            remote(summed.at[i % 2], back.at[i], back_s.at[i], back_r.at[i], lo_peer).start()

    def add_last(h, c):
        @pl.loop(h * QUARTER, (h + 1) * QUARTER)
        def _(z):
            here = pl.ds(c * HALF + z, ROWS, stride=ZS)
            term = y_result[LAST, core, z] if c is core else y_got[LAST, 0, z]
            turn[here] = turn[here] + term.astype(F32)

    def finish_last():
        for h in range(2):
            drain(y_got.at[LAST, 0, pl.ds(0, QUARTER)], last_ys_r.at[h])
            add_last(h, other_core)
        drain(z_last, zo_r.at[LAST, lo])

        @pl.loop(0, ROWS // 16)
        def _(j):
            rows = pl.ds(j * 16, 16)
            total[rows, :, lanes(mine, LAST)] = (sixteen(turn, j) + z_last[rows].astype(F32)).astype(BF16)

    def finish(i):
        if i != LAST:
            x_fetch(i, False).start()
        drain(back.at[i], back_r.at[i])
        x_fetch(i, False).wait()

        @pl.loop(0, ROWS // 16)
        def _(j):
            rows = pl.ds(j * 16, 16)
            total[rows, :, lanes(theirs, i)] = (back[i, rows].astype(F32) + sixteen(x_got, j)).astype(BF16)

    def take(i):
        drain(traded.at[i], lo_r.at[i])
        send_z(i, False)
        send_y(i, False)

    for i in range(CHUNKS):
        remote(field.at[:, :, lanes(theirs, i)], traded.at[i], lo_s.at[i], lo_r.at[i], lo_peer).start()
    send_y(0, True)
    send_z(0, True)
    send_z(1, True)
    send_z(2, True)
    for i in range(1, CHUNKS):
        send_y(i, True)
    loads[0].wait()
    do_x(0, 8)
    take(0)
    make_y_op()
    make_z_op()
    do_y(0, False)
    do_x(8, 13)
    take(1)
    do_z(0)
    return_z(0, False)
    send_z(3, True)
    do_y(1, False)
    do_x(13, 18)
    take(2)
    do_z(1)
    return_z(1, False)
    combine(0, False)
    do_y(2, False)
    do_x(18, 21)
    take(3)
    do_z(2)
    return_z(2, False)
    combine(1, False)
    do_x(21, 24)
    do_z(3)
    return_z(3, False)
    for i in range(CHUNKS):
        return_z(i, True)
    for slot in range(2):
        x_store(slot, slot).wait()
    do_y(3, False)
    finish(0)
    do_y(0, True)
    combine(2, False)
    combine(3, False)
    finish(1)
    do_y(1, True)
    combine(0, True)
    finish(2)
    do_y(2, True)
    combine(1, True)
    do_y_last(0)
    combine(2, True)
    x_fetch(LAST, False).start()
    x_last = pltpu.make_async_copy(x_term.at[upper * CHUNKS + LAST], turn, load)
    x_last.start()
    x_last.wait()
    add_last(0, core)
    do_y_last(1)
    finish(LAST)
    add_last(1, core)
    finish_last()

    for i in range(CHUNKS):
        drain(traded.at[i], lo_s.at[i])
        for part in range(2):
            drain(z_in.at[i, :, pl.ds(0, PLANE - 1), 0], zi_s.at[i, part])
        for n in range(3):
            drain(staged.at[i, pl.ds(0, HALF)], g_s.at[i, 1, n])
        for half in range(2):
            drain(z_out.at[i, half, pl.ds(0, (PLANE - 1) * YS)], zo_s.at[i, half])
        if i != LAST:
            drain(y_got.at[i, 0], ys_s.at[i, 0])
        if i >= 2:
            drain(summed.at[i % 2], back_s.at[i])
    for n in range(2):
        drain(y_got.at[LAST, 0, pl.ds(0, QUARTER)], last_ys_s.at[n])


def laplacian(*operands):
    any_space, vmem = pl.BlockSpec(memory_space=pl.ANY), pl.BlockSpec(memory_space=pltpu.VMEM)
    shape = lambda *dims: jax.ShapeDtypeStruct(dims, BF16)
    held = lambda *dims: pltpu.VMEM(dims, BF16)
    dma = pltpu.SemaphoreType.DMA
    nx = 2 * CHUNKS * LANES
    return pl.pallas_call(
        laplacian_kernel,
        name="laplacian",
        out_shape=(
            held(ROWS, ZS, nx),
            shape(CHUNKS, ROWS, ZS, LANES),
            shape(CHUNKS, YS, PLANE, 2, ZS, LANES),
            shape(CHUNKS, 2, HALF, 4, ROWS, LANES),
            shape(CHUNKS, 2, ROWS, ZS, LANES),
            jax.ShapeDtypeStruct((2 * CHUNKS, ROWS * ZS, LANES), F32),
        ),
        in_specs=[any_space] * 4 + [vmem] * 2 + [any_space],
        out_specs=(vmem,) + (any_space,) * 5,
        scratch_shapes=[
            held(nx, nx), held(2, NY, 2 * ROWS), held(2 * ROWS, NY), held(NZ, NZ), held(NZ, NZ),
            held(2, XS, ZS, nx),
            pltpu.VMEM((2, 2 * CHUNKS, XS * ZS, LANES), F32),
            pltpu.VMEM((ROWS * ZS, LANES), F32),
            pltpu.VMEM((ROWS * ZS, LANES), F32),
            held(CHUNKS, ZS, ROWS, LANES),
            held(ROWS, ZS, LANES),
            held(YS, PLANE, 2, ZS, LANES),
            held(CHUNKS, YS, PLANE, 2, ZS, LANES),
            held(HALF, 4, ROWS, LANES),
            held(CHUNKS, 2, HALF, ROWS, LANES),
            held(CHUNKS, 2, HALF, ROWS, LANES),
            held(ROWS, ZS, LANES),
            held(2, ROWS, ZS, LANES),
            held(CHUNKS, ROWS, ZS, LANES), held(HALF, 4, ROWS, LANES), held(ROWS, ZS, LANES),
            dma((CHUNKS,)), dma((CHUNKS,)),
            dma((CHUNKS, 2)), dma((CHUNKS,)),
            dma((CHUNKS, 2, 3)), dma((CHUNKS, 2)), dma((CHUNKS, 2)),
            dma((CHUNKS, 2)), dma((CHUNKS, 2)),
            dma((CHUNKS, 2)), dma((CHUNKS, 2)),
            dma((CHUNKS,)), dma((CHUNKS,)),
            dma, dma((4,)), dma((2,)), dma((2,)), dma,
            dma, dma((2,)), dma((2,)), dma((2,)),
        ],
        compiler_params=pltpu.CompilerParams(
            collective_id=0, has_side_effects=True, vmem_limit_bytes=54 * 2**20
        ),
        cost_estimate=pl.CostEstimate(flops=24_200_000_000, bytes_accessed=180_000_000, transcendentals=0),
    )(*operands)[0]


def write_kernel(source, target, sems):
    parts = sems.shape[0]
    rows = source.shape[0] // parts
    copies = [
        pltpu.make_async_copy(source.at[pl.ds(n * rows, rows)], target.at[pl.ds(n * rows, rows)], sems.at[n])
        for n in range(parts)
    ]
    for copy in copies:
        copy.start()
    for copy in copies:
        copy.wait()


def written(array):
    return pl.pallas_call(
        write_kernel,
        name="result",
        in_specs=[pl.BlockSpec(memory_space=pltpu.VMEM)],
        out_specs=pl.BlockSpec(memory_space=pl.ANY),
        out_shape=jax.ShapeDtypeStruct(array.shape, array.dtype),
        scratch_shapes=[pltpu.SemaphoreType.DMA((4,))],
        compiler_params=pltpu.CompilerParams(vmem_limit_bytes=16 * 2**20),
    )(array)


def per_device(scalar_field, x_operator, y_second, y_first, y_stretch, y_curve, z_operator):
    return written(laplacian(
        scalar_field, x_operator, y_second, y_first, y_stretch, y_curve, z_operator
    ))


def solution(mesh):
    in_specs = (P("row", "col", None), P(), P(), P(), P(), P(), P())
    out_specs = P("row", "col", None)
    return jax.shard_map(
        per_device, mesh=mesh, in_specs=in_specs, out_specs=out_specs, check_vma=False
    )
```

```python
import jax
import jax.numpy as jnp
from jax import lax
from jax.experimental import pallas as pl
from jax.experimental.pallas import tpu as pltpu
from jax.sharding import PartitionSpec as P

MESH = pl.DeviceIdType.MESH
BF16 = jnp.bfloat16
F32 = jnp.float32
LANES = 128
CHUNKS = 4
PLANE = 16
ROWS = 192
ZS = 24
YS = ROWS // PLANE
HALF = ZS // 2
QUARTER = HALF // 2
LAST = CHUNKS - 1
XS = 8
NY = 4 * ROWS
NZ = 2 * PLANE * ZS


def laplacian_kernel(
    field, x_source, y_second, y_first, y_stretch, y_curve, z_source,
    total, traded, z_in, y_in, z_out, x_term,
    x_op, y_parts, y_op, z_raw, z_op, x_tile, x_result, x_got,
    turn, staged, block, z_pencil, z_result, y_pencil, y_result, y_got, z_got, summed,
    back, y_last, z_last,
    lo_s, lo_r, zi_s, zi_r, g_s, g_l, g_r, zo_s, zo_r, ys_s, ys_r, back_s, back_r, load, ops_l, x_l, x_s,
    x_g, z_l, last_r, last_ys_s, last_ys_r,
):
    row, col = lax.axis_index("row"), lax.axis_index("col")
    hi, core = row // 2, row % 2
    plane, lo = col // 2, col % 2
    pz, py = plane // 4, plane % 4
    upper = 1 - lax.rem(hi + lo, 2)
    mine, theirs = upper * (CHUNKS * LANES), (1 - upper) * (CHUNKS * LANES)
    other_lo, other_core = 1 - lo, 1 - core

    lo_peer = (row, plane * 2 + other_lo)
    sibling = (hi * 2 + 1 - core, col)
    far_same = ((1 - hi) * 2 + core, plane * 2 + other_lo)
    far_cross = ((1 - hi) * 2 + 1 - core, plane * 2 + other_lo)

    def plane_peer(k):
        k = lax.rem(k * 7, PLANE)
        return lax.rem(pz + k // 4, 4) * 4 + lax.rem(py + k % 4, 4)

    def lanes(start, i):
        return pl.ds(pl.multiple_of(start + i * LANES, LANES), LANES)

    def remote(src, dst, send, recv, device):
        return pltpu.make_async_remote_copy(
            src_ref=src, dst_ref=dst, send_sem=send, recv_sem=recv, device_id=device, device_id_type=MESH
        )

    def drain(ref, sem):
        pltpu.make_async_copy(ref, ref, sem).wait()

    def fetch(src, dst):
        copy = pltpu.make_async_copy(src, dst, load)
        copy.start()
        copy.wait()

    y_columns = pl.ds(pl.multiple_of(hi * (2 * ROWS), LANES), 2 * ROWS)
    loads = [
        pltpu.make_async_copy(source, target, ops_l.at[n])
        for n, (source, target) in enumerate((
            (x_source, x_op), (y_second.at[:, y_columns], y_parts.at[0]),
            (y_first.at[:, y_columns], y_parts.at[1]), (z_source, z_raw),
        ))
    ]
    for copy in loads:
        copy.start()

    def x_load(j, slot):
        return pltpu.make_async_copy(field.at[pl.ds(j * XS, XS)], x_tile.at[slot], x_l.at[slot])

    first_block = pltpu.make_async_copy(field.at[:, :, lanes(mine, 0)], block, load)
    first_block.start()
    x_load(0, 0).start()

    barrier = pltpu.get_barrier_semaphore()
    for peer in (lo_peer, sibling, far_same, far_cross):
        pl.semaphore_signal(barrier, inc=1, device_id=peer, device_id_type=MESH)

    @pl.loop(1, PLANE)
    def _(k):
        pl.semaphore_signal(barrier, inc=1, device_id=(row, plane_peer(k) * 2 + lo), device_id_type=MESH)

    def turn_block(i):
        @pl.loop(0, ROWS // 16)
        def _(j):
            turn[pl.ds(j * 16 * ZS, 16 * ZS)] = block[pl.ds(j * 16, 16)].astype(F32).reshape(16 * ZS, LANES)

        @pl.loop(0, ZS)
        def _(z):
            staged[i, z] = turn[pl.ds(z, ROWS, stride=ZS)].astype(BF16)

    first_block.wait()
    turn_block(0)
    pl.semaphore_wait(barrier, 4 + PLANE - 1)

    def part_of(i, own):
        return field.at[:, :, lanes(mine, i)] if own else traded.at[i]

    def send_z(i, own):
        source = part_of(i, own)
        z_half = lo if own else other_lo
        part = 0 if own else 1

        @pl.loop(1, PLANE)
        def _(k):
            to = plane_peer(k)
            remote(
                source.at[pl.ds(to * YS, YS)], z_in.at[i, :, plane, z_half],
                zi_s.at[i, part], zi_r.at[i], (row, to * 2 + lo),
            ).start()

        pltpu.make_async_copy(
            source.at[pl.ds(plane * YS, YS)], z_in.at[i, :, plane, z_half], zi_r.at[i]
        ).start()

    def y_target(i, z_half, own, source_row):
        held = y_last if i == LAST and own else y_in.at[i, z_half]
        return held.at[:, source_row]

    def z_target(i, half, own):
        return z_last if i == LAST and own else z_out.at[i, half]

    def send_y(i, own):
        part, z_half = (0, lo) if own else (1, other_lo)
        if not own:
            drain(staged.at[i, pl.ds(0, HALF)], g_l.at[i, 0])
            for n in range(3):
                drain(staged.at[i, pl.ds(0, HALF)], g_s.at[i, 0, n])
        if not (own and i == 0):
            fetch(part_of(i, own), block)

        if not (own and i == 0):
            turn_block(i)

        keep, give = core * HALF, (1 - core) * HALF
        whole = pl.ds(0, HALF)
        near = y_target(i, z_half, own, row)
        far = y_target(i, z_half, not own, row)
        pieces = [(keep, far_same, 0, far), (give, far_cross, 1, far), (give, sibling, 2, near)]
        if i == LAST and not own:
            for h in range(2):
                for z, peer, n, target in pieces[:2]:
                    remote(
                        staged.at[i, pl.ds(z + h * QUARTER, QUARTER)], target.at[pl.ds(h * QUARTER, QUARTER)],
                        g_s.at[i, part, n], last_r.at[h], peer,
                    ).start()
            pieces = pieces[2:]
        for z, peer, n, target in pieces:
            remote(
                staged.at[i, pl.ds(z, HALF)], target.at[whole], g_s.at[i, part, n], g_r.at[i, z_half], peer
            ).start()
        pltpu.make_async_copy(staged.at[i, pl.ds(keep, HALF)], near.at[whole], g_l.at[i, part]).start()

    def do_z(i):
        drain(z_in.at[i], zi_r.at[i])
        fetch(z_in.at[i], z_pencil)

        @pl.loop(0, YS // 2)
        def _(j):
            def points(y):
                return z_pencil[y].astype(F32).reshape(NZ, LANES).astype(BF16)

            pair = jnp.concatenate([points(2 * j), points(2 * j + 1)], axis=1)
            product = jnp.dot(z_op[...], pair, preferred_element_type=F32)
            for n in range(2):
                result = product[:, n * LANES:(n + 1) * LANES].reshape(PLANE, 2, ZS, LANES)
                z_result[i, 2 * j + n] = result.astype(BF16)

    def return_z(i, own):
        half = lo if own else other_lo
        target = z_target(i, half, own).at[pl.ds(plane * YS, YS)]

        @pl.loop(1, PLANE)
        def _(k):
            to = plane_peer(k)
            remote(
                z_result.at[i, :, to, half], target,
                zo_s.at[i, half], zo_r.at[i, half], (row, to * 2 + lo),
            ).start()

        pltpu.make_async_copy(
            z_result.at[i, :, plane, half], target, zo_r.at[i, half]
        ).start()

    def make_y_op():
        loads[1].wait()
        loads[2].wait()
        for n in range(3):
            here = slice(n * LANES, (n + 1) * LANES)
            there = pl.ds(pl.multiple_of(hi * (2 * ROWS) + n * LANES, LANES), LANES)
            combined = (
                y_stretch[there].reshape(1, LANES) * y_parts[0, :, here].astype(F32)
                + y_curve[there].reshape(1, LANES) * y_parts[1, :, here].astype(F32)
            )
            y_op[here] = combined.T.astype(BF16)

    def make_z_op():
        loads[3].wait()
        for n in range(NZ // LANES):
            here = slice(n * LANES, (n + 1) * LANES)
            z_op[here] = z_raw[:, here].astype(F32).T.astype(BF16)

    def x_store(j, slot):
        return pltpu.make_async_copy(x_result.at[slot], x_term.at[:, pl.ds(j * (XS * ZS), XS * ZS)], x_s.at[slot])

    def do_x(first, last):
        @pl.loop(first, last)
        def _(j):
            slot = lax.rem(j, 2)
            x_load(j, slot).wait()

            @pl.when(j + 1 < ROWS // XS)
            def _():
                x_load(j + 1, 1 - slot).start()

            @pl.when(j >= 2)
            def _():
                x_store(j - 2, slot).wait()

            flat = x_tile[slot].reshape(XS * ZS, 2 * CHUNKS * LANES)
            product = jnp.dot(flat, x_op[...], preferred_element_type=F32)
            for n in range(2 * CHUNKS):
                x_result[slot, n] = product[:, n * LANES:(n + 1) * LANES]
            x_store(j, slot).start()

    def y_products(i, held, first, last):
        @pl.loop(first, last)
        def _(j):
            pair = jnp.concatenate([held[2 * j].reshape(NY, LANES), held[2 * j + 1].reshape(NY, LANES)], axis=1)
            product = jnp.dot(y_op[...], pair, preferred_element_type=F32).astype(BF16)
            for n in range(2):
                for c in range(2):
                    y_result[i, c, 2 * j + n] = product[c * ROWS:(c + 1) * ROWS, n * LANES:(n + 1) * LANES]

    def do_y(i, own):
        part, half = (0, lo) if own else (1, other_lo)
        drain(y_in.at[i, half, :, pl.ds(0, 3)], g_r.at[i, half])
        if own:
            drain(y_got.at[i, 1], ys_s.at[i, 1])
        else:
            drain(staged.at[i, pl.ds(0, HALF)], g_l.at[i, 1])
        fetch(y_in.at[i, half], y_pencil)
        y_products(i, y_pencil, 0, HALF // 2)
        remote(
            y_result.at[i, 1 - core], y_got.at[i, part], ys_s.at[i, part], ys_r.at[i, part], sibling
        ).start()

    def do_y_last(h):
        if h == 0:
            drain(y_got.at[LAST, 1], ys_s.at[LAST, 1])
            drain(y_last.at[:, 0], g_r.at[LAST, lo])
        drain(y_last.at[pl.ds(0, QUARTER), pl.ds(0, 2)], last_r.at[h])
        y_products(LAST, y_last, h * (QUARTER // 2), (h + 1) * (QUARTER // 2))
        piece = pl.ds(h * QUARTER, QUARTER)
        remote(
            y_result.at[LAST, 1 - core, piece], y_got.at[LAST, 0, piece], last_ys_s.at[h], last_ys_r.at[h], sibling
        ).start()

    def x_fetch(i, own):
        return pltpu.make_async_copy(x_term.at[(upper if own else 1 - upper) * CHUNKS + i], x_got, x_g)

    def sixteen(ref, j):
        return ref[pl.ds(j * (16 * ZS), 16 * ZS)].reshape(16, ZS, LANES)

    def combine(i, own):
        part, half = (0, lo) if own else (1, other_lo)
        if own:
            x_fetch(i, True).start()

        @pl.loop(0, HALF)
        def _(z):
            turn[pl.ds(core * HALF + z, ROWS, stride=ZS)] = y_result[i, core, z].astype(F32)

        drain(z_out.at[i, half], zo_r.at[i, half])
        z_fetch = pltpu.make_async_copy(z_out.at[i, half], z_got, z_l)
        z_fetch.start()
        drain(y_got.at[i, part], ys_r.at[i, part])

        @pl.loop(0, HALF)
        def _(z):
            turn[pl.ds((1 - core) * HALF + z, ROWS, stride=ZS)] = y_got[i, part, z].astype(F32)

        if own:
            x_fetch(i, True).wait()
        elif i >= 2:
            drain(summed.at[i % 2], back_s.at[i - 2])
        z_fetch.wait()

        @pl.loop(0, ROWS // 16)
        def _(j):
            rows = pl.ds(j * 16, 16)
            both = sixteen(turn, j) + z_got[rows].astype(F32)
            if own:
                total[rows, :, lanes(mine, i)] = (both + sixteen(x_got, j)).astype(BF16)
            else:
                summed[i % 2, rows] = both.astype(BF16)

        if not own:
            remote(summed.at[i % 2], back.at[i], back_s.at[i], back_r.at[i], lo_peer).start()

    def add_last(h, c):
        @pl.loop(h * QUARTER, (h + 1) * QUARTER)
        def _(z):
            here = pl.ds(c * HALF + z, ROWS, stride=ZS)
            term = y_result[LAST, core, z] if c is core else y_got[LAST, 0, z]
            turn[here] = turn[here] + term.astype(F32)

    def finish_last():
        for h in range(2):
            drain(y_got.at[LAST, 0, pl.ds(0, QUARTER)], last_ys_r.at[h])
            add_last(h, other_core)
        drain(z_last, zo_r.at[LAST, lo])

        @pl.loop(0, ROWS // 16)
        def _(j):
            rows = pl.ds(j * 16, 16)
            total[rows, :, lanes(mine, LAST)] = (sixteen(turn, j) + z_last[rows].astype(F32)).astype(BF16)

    def finish(i):
        if i != LAST:
            x_fetch(i, False).start()
        drain(back.at[i], back_r.at[i])
        x_fetch(i, False).wait()

        @pl.loop(0, ROWS // 16)
        def _(j):
            rows = pl.ds(j * 16, 16)
            total[rows, :, lanes(theirs, i)] = (back[i, rows].astype(F32) + sixteen(x_got, j)).astype(BF16)

    def take(i):
        drain(traded.at[i], lo_r.at[i])
        send_z(i, False)
        send_y(i, False)

    for i in range(CHUNKS):
        remote(field.at[:, :, lanes(theirs, i)], traded.at[i], lo_s.at[i], lo_r.at[i], lo_peer).start()
    send_y(0, True)
    send_z(0, True)
    send_z(1, True)
    send_z(2, True)
    for i in range(1, CHUNKS):
        send_y(i, True)
    loads[0].wait()
    do_x(0, 8)
    take(0)
    make_y_op()
    make_z_op()
    do_y(0, False)
    do_x(8, 13)
    take(1)
    do_z(0)
    return_z(0, False)
    send_z(3, True)
    do_y(1, False)
    do_x(13, 18)
    take(2)
    do_z(1)
    return_z(1, False)
    combine(0, False)
    do_y(2, False)
    do_x(18, 21)
    take(3)
    do_z(2)
    return_z(2, False)
    combine(1, False)
    do_x(21, 24)
    do_z(3)
    return_z(3, False)
    for i in range(CHUNKS):
        return_z(i, True)
    for slot in range(2):
        x_store(slot, slot).wait()
    do_y(3, False)
    finish(0)
    do_y(0, True)
    combine(2, False)
    combine(3, False)
    finish(1)
    do_y(1, True)
    combine(0, True)
    finish(2)
    do_y(2, True)
    combine(1, True)
    do_y_last(0)
    combine(2, True)
    x_fetch(LAST, False).start()
    x_last = pltpu.make_async_copy(x_term.at[upper * CHUNKS + LAST], turn.at[pl.ds(0, ROWS * ZS)], load)
    x_last.start()
    x_last.wait()
    add_last(0, core)
    do_y_last(1)
    finish(LAST)
    add_last(1, core)
    finish_last()

    for i in range(CHUNKS):
        drain(traded.at[i], lo_s.at[i])
        for part in range(2):
            drain(z_in.at[i, :, pl.ds(0, PLANE - 1), 0], zi_s.at[i, part])
        for n in range(3):
            drain(staged.at[i, pl.ds(0, HALF)], g_s.at[i, 1, n])
        for half in range(2):
            drain(z_out.at[i, half, pl.ds(0, (PLANE - 1) * YS)], zo_s.at[i, half])
        if i != LAST:
            drain(y_got.at[i, 0], ys_s.at[i, 0])
        if i >= 2:
            drain(summed.at[i % 2], back_s.at[i])
    for n in range(2):
        drain(y_got.at[LAST, 0, pl.ds(0, QUARTER)], last_ys_s.at[n])


def laplacian(*operands):
    any_space, vmem = pl.BlockSpec(memory_space=pl.ANY), pl.BlockSpec(memory_space=pltpu.VMEM)
    shape = lambda *dims: jax.ShapeDtypeStruct(dims, BF16)
    held = lambda *dims: pltpu.VMEM(dims, BF16)
    dma = pltpu.SemaphoreType.DMA
    nx = 2 * CHUNKS * LANES
    return pl.pallas_call(
        laplacian_kernel,
        name="laplacian",
        out_shape=(
            held(ROWS, ZS, nx),
            shape(CHUNKS, ROWS, ZS, LANES),
            shape(CHUNKS, YS, PLANE, 2, ZS, LANES),
            shape(CHUNKS, 2, HALF, 4, ROWS, LANES),
            shape(CHUNKS, 2, ROWS, ZS, LANES),
            jax.ShapeDtypeStruct((2 * CHUNKS, ROWS * ZS, LANES), F32),
        ),
        in_specs=[any_space] * 4 + [vmem] * 2 + [any_space],
        out_specs=(vmem,) + (any_space,) * 5,
        scratch_shapes=[
            held(nx, nx), held(2, NY, 2 * ROWS), held(2 * ROWS, NY), held(NZ, NZ), held(NZ, NZ),
            held(2, XS, ZS, nx),
            pltpu.VMEM((2, 2 * CHUNKS, XS * ZS, LANES), F32),
            pltpu.VMEM((ROWS * ZS, LANES), F32),
            pltpu.VMEM((ROWS * ZS + ZS, LANES), F32),
            held(CHUNKS, ZS, ROWS, LANES),
            held(ROWS, ZS, LANES),
            held(YS, PLANE, 2, ZS, LANES),
            held(CHUNKS, YS, PLANE, 2, ZS, LANES),
            held(HALF, 4, ROWS, LANES),
            held(CHUNKS, 2, HALF, ROWS, LANES),
            held(CHUNKS, 2, HALF, ROWS, LANES),
            held(ROWS, ZS, LANES),
            held(2, ROWS, ZS, LANES),
            held(CHUNKS, ROWS, ZS, LANES), held(HALF, 4, ROWS, LANES), held(ROWS, ZS, LANES),
            dma((CHUNKS,)), dma((CHUNKS,)),
            dma((CHUNKS, 2)), dma((CHUNKS,)),
            dma((CHUNKS, 2, 3)), dma((CHUNKS, 2)), dma((CHUNKS, 2)),
            dma((CHUNKS, 2)), dma((CHUNKS, 2)),
            dma((CHUNKS, 2)), dma((CHUNKS, 2)),
            dma((CHUNKS,)), dma((CHUNKS,)),
            dma, dma((4,)), dma((2,)), dma((2,)), dma,
            dma, dma((2,)), dma((2,)), dma((2,)),
        ],
        compiler_params=pltpu.CompilerParams(
            collective_id=0, has_side_effects=True, vmem_limit_bytes=54 * 2**20
        ),
        cost_estimate=pl.CostEstimate(flops=24_200_000_000, bytes_accessed=180_000_000, transcendentals=0),
    )(*operands)[0]


def write_kernel(source, target, sems):
    parts = sems.shape[0]
    rows = source.shape[0] // parts
    copies = [
        pltpu.make_async_copy(source.at[pl.ds(n * rows, rows)], target.at[pl.ds(n * rows, rows)], sems.at[n])
        for n in range(parts)
    ]
    for copy in copies:
        copy.start()
    for copy in copies:
        copy.wait()


def written(array):
    return pl.pallas_call(
        write_kernel,
        name="result",
        in_specs=[pl.BlockSpec(memory_space=pltpu.VMEM)],
        out_specs=pl.BlockSpec(memory_space=pl.ANY),
        out_shape=jax.ShapeDtypeStruct(array.shape, array.dtype),
        scratch_shapes=[pltpu.SemaphoreType.DMA((4,))],
        compiler_params=pltpu.CompilerParams(vmem_limit_bytes=16 * 2**20),
    )(array)


def per_device(scalar_field, x_operator, y_second, y_first, y_stretch, y_curve, z_operator):
    return written(laplacian(
        scalar_field, x_operator, y_second, y_first, y_stretch, y_curve, z_operator
    ))


def solution(mesh):
    in_specs = (P("row", "col", None), P(), P(), P(), P(), P(), P())
    out_specs = P("row", "col", None)
    return jax.shard_map(
        per_device, mesh=mesh, in_specs=in_specs, out_specs=out_specs, check_vma=False
    )
```

```python
import jax
import jax.numpy as jnp
from jax import lax
from jax.experimental import pallas as pl
from jax.experimental.pallas import tpu as pltpu
from jax.sharding import PartitionSpec as P

MESH = pl.DeviceIdType.MESH
BF16 = jnp.bfloat16
F32 = jnp.float32
LANES = 128
CHUNKS = 4
PLANE = 16
ROWS = 192
ZS = 24
YS = ROWS // PLANE
HALF = ZS // 2
PIECES = 3
PIECE = HALF // PIECES
LAST = CHUNKS - 1
XS = 8
NY = 4 * ROWS
NZ = 2 * PLANE * ZS


def laplacian_kernel(
    field, x_source, y_second, y_first, y_stretch, y_curve, z_source,
    total, traded, z_in, y_in, z_out, x_term,
    x_op, y_parts, y_op, z_raw, z_op, x_tile, x_result, x_got,
    turn, staged, block, z_pencil, z_result, y_pencil, y_result, y_got, z_got, summed,
    back, y_last, z_last,
    lo_s, lo_r, zi_s, zi_r, g_s, g_l, g_r, zo_s, zo_r, ys_s, ys_r, back_s, back_r, load, ops_l, x_l, x_s,
    x_g, z_l, last_r, last_ys_s, last_ys_r,
):
    row, col = lax.axis_index("row"), lax.axis_index("col")
    hi, core = row // 2, row % 2
    plane, lo = col // 2, col % 2
    pz, py = plane // 4, plane % 4
    upper = 1 - lax.rem(hi + lo, 2)
    mine, theirs = upper * (CHUNKS * LANES), (1 - upper) * (CHUNKS * LANES)
    other_lo, other_core = 1 - lo, 1 - core

    lo_peer = (row, plane * 2 + other_lo)
    sibling = (hi * 2 + 1 - core, col)
    far_same = ((1 - hi) * 2 + core, plane * 2 + other_lo)
    far_cross = ((1 - hi) * 2 + 1 - core, plane * 2 + other_lo)

    def plane_peer(k):
        k = lax.rem(k * 7, PLANE)
        return lax.rem(pz + k // 4, 4) * 4 + lax.rem(py + k % 4, 4)

    def lanes(start, i):
        return pl.ds(pl.multiple_of(start + i * LANES, LANES), LANES)

    def remote(src, dst, send, recv, device):
        return pltpu.make_async_remote_copy(
            src_ref=src, dst_ref=dst, send_sem=send, recv_sem=recv, device_id=device, device_id_type=MESH
        )

    def drain(ref, sem):
        pltpu.make_async_copy(ref, ref, sem).wait()

    def fetch(src, dst):
        copy = pltpu.make_async_copy(src, dst, load)
        copy.start()
        copy.wait()

    y_columns = pl.ds(pl.multiple_of(hi * (2 * ROWS), LANES), 2 * ROWS)
    loads = [
        pltpu.make_async_copy(source, target, ops_l.at[n])
        for n, (source, target) in enumerate((
            (x_source, x_op), (y_second.at[:, y_columns], y_parts.at[0]),
            (y_first.at[:, y_columns], y_parts.at[1]), (z_source, z_raw),
        ))
    ]
    for copy in loads:
        copy.start()

    def x_load(j, slot):
        return pltpu.make_async_copy(field.at[pl.ds(j * XS, XS)], x_tile.at[slot], x_l.at[slot])

    first_block = pltpu.make_async_copy(field.at[:, :, lanes(mine, 0)], block, load)
    first_block.start()
    x_load(0, 0).start()

    barrier = pltpu.get_barrier_semaphore()
    for peer in (lo_peer, sibling, far_same, far_cross):
        pl.semaphore_signal(barrier, inc=1, device_id=peer, device_id_type=MESH)

    @pl.loop(1, PLANE)
    def _(k):
        pl.semaphore_signal(barrier, inc=1, device_id=(row, plane_peer(k) * 2 + lo), device_id_type=MESH)

    def turn_block(i):
        @pl.loop(0, ROWS // 16)
        def _(j):
            turn[pl.ds(j * 16 * ZS, 16 * ZS)] = block[pl.ds(j * 16, 16)].astype(F32).reshape(16 * ZS, LANES)

        @pl.loop(0, ZS)
        def _(z):
            staged[i, z] = turn[pl.ds(z, ROWS, stride=ZS)].astype(BF16)

    first_block.wait()
    turn_block(0)
    pl.semaphore_wait(barrier, 4 + PLANE - 1)

    def part_of(i, own):
        return field.at[:, :, lanes(mine, i)] if own else traded.at[i]

    def send_z(i, own):
        source = part_of(i, own)
        z_half = lo if own else other_lo
        part = 0 if own else 1

        @pl.loop(1, PLANE)
        def _(k):
            to = plane_peer(k)
            remote(
                source.at[pl.ds(to * YS, YS)], z_in.at[i, :, plane, z_half],
                zi_s.at[i, part], zi_r.at[i], (row, to * 2 + lo),
            ).start()

        pltpu.make_async_copy(
            source.at[pl.ds(plane * YS, YS)], z_in.at[i, :, plane, z_half], zi_r.at[i]
        ).start()

    def y_target(i, z_half, own, source_row):
        held = y_last if i == LAST and own else y_in.at[i, z_half]
        return held.at[:, source_row]

    def z_target(i, half, own):
        return z_last if i == LAST and own else z_out.at[i, half]

    def send_y(i, own):
        part, z_half = (0, lo) if own else (1, other_lo)
        if not own:
            drain(staged.at[i, pl.ds(0, HALF)], g_l.at[i, 0])
            for n in range(3):
                drain(staged.at[i, pl.ds(0, HALF)], g_s.at[i, 0, n])
        if not (own and i == 0):
            fetch(part_of(i, own), block)

        if not (own and i == 0):
            turn_block(i)

        keep, give = core * HALF, (1 - core) * HALF
        whole = pl.ds(0, HALF)
        near = y_target(i, z_half, own, row)
        far = y_target(i, z_half, not own, row)
        pieces = [(keep, far_same, 0, far), (give, far_cross, 1, far), (give, sibling, 2, near)]
        if i == LAST and not own:
            for h in range(PIECES):
                for z, peer, n, target in pieces[:2]:
                    remote(
                        staged.at[i, pl.ds(z + h * PIECE, PIECE)], target.at[pl.ds(h * PIECE, PIECE)],
                        g_s.at[i, part, n], last_r.at[h], peer,
                    ).start()
            pieces = pieces[2:]
        for z, peer, n, target in pieces:
            remote(
                staged.at[i, pl.ds(z, HALF)], target.at[whole], g_s.at[i, part, n], g_r.at[i, z_half], peer
            ).start()
        pltpu.make_async_copy(staged.at[i, pl.ds(keep, HALF)], near.at[whole], g_l.at[i, part]).start()

    def do_z(i):
        drain(z_in.at[i], zi_r.at[i])
        fetch(z_in.at[i], z_pencil)

        @pl.loop(0, YS // 2)
        def _(j):
            def points(y):
                return z_pencil[y].astype(F32).reshape(NZ, LANES).astype(BF16)

            pair = jnp.concatenate([points(2 * j), points(2 * j + 1)], axis=1)
            product = jnp.dot(z_op[...], pair, preferred_element_type=F32)
            for n in range(2):
                result = product[:, n * LANES:(n + 1) * LANES].reshape(PLANE, 2, ZS, LANES)
                z_result[i, 2 * j + n] = result.astype(BF16)

    def return_z(i, own):
        half = lo if own else other_lo
        target = z_target(i, half, own).at[pl.ds(plane * YS, YS)]

        @pl.loop(1, PLANE)
        def _(k):
            to = plane_peer(k)
            remote(
                z_result.at[i, :, to, half], target,
                zo_s.at[i, half], zo_r.at[i, half], (row, to * 2 + lo),
            ).start()

        pltpu.make_async_copy(
            z_result.at[i, :, plane, half], target, zo_r.at[i, half]
        ).start()

    def make_y_op():
        loads[1].wait()
        loads[2].wait()
        for n in range(3):
            here = slice(n * LANES, (n + 1) * LANES)
            there = pl.ds(pl.multiple_of(hi * (2 * ROWS) + n * LANES, LANES), LANES)
            combined = (
                y_stretch[there].reshape(1, LANES) * y_parts[0, :, here].astype(F32)
                + y_curve[there].reshape(1, LANES) * y_parts[1, :, here].astype(F32)
            )
            y_op[here] = combined.T.astype(BF16)

    def make_z_op():
        loads[3].wait()
        for n in range(NZ // LANES):
            here = slice(n * LANES, (n + 1) * LANES)
            z_op[here] = z_raw[:, here].astype(F32).T.astype(BF16)

    def x_store(j, slot):
        return pltpu.make_async_copy(x_result.at[slot], x_term.at[:, pl.ds(j * (XS * ZS), XS * ZS)], x_s.at[slot])

    def do_x(first, last):
        @pl.loop(first, last)
        def _(j):
            slot = lax.rem(j, 2)
            x_load(j, slot).wait()

            @pl.when(j + 1 < ROWS // XS)
            def _():
                x_load(j + 1, 1 - slot).start()

            @pl.when(j >= 2)
            def _():
                x_store(j - 2, slot).wait()

            flat = x_tile[slot].reshape(XS * ZS, 2 * CHUNKS * LANES)
            product = jnp.dot(flat, x_op[...], preferred_element_type=F32)
            for n in range(2 * CHUNKS):
                x_result[slot, n] = product[:, n * LANES:(n + 1) * LANES]
            x_store(j, slot).start()

    def y_products(i, held, first, last):
        @pl.loop(first, last)
        def _(j):
            pair = jnp.concatenate([held[2 * j].reshape(NY, LANES), held[2 * j + 1].reshape(NY, LANES)], axis=1)
            product = jnp.dot(y_op[...], pair, preferred_element_type=F32).astype(BF16)
            for n in range(2):
                for c in range(2):
                    y_result[i, c, 2 * j + n] = product[c * ROWS:(c + 1) * ROWS, n * LANES:(n + 1) * LANES]

    def do_y(i, own):
        part, half = (0, lo) if own else (1, other_lo)
        drain(y_in.at[i, half, :, pl.ds(0, 3)], g_r.at[i, half])
        if own:
            drain(y_got.at[i, 1], ys_s.at[i, 1])
        else:
            drain(staged.at[i, pl.ds(0, HALF)], g_l.at[i, 1])
        fetch(y_in.at[i, half], y_pencil)
        y_products(i, y_pencil, 0, HALF // 2)
        remote(
            y_result.at[i, 1 - core], y_got.at[i, part], ys_s.at[i, part], ys_r.at[i, part], sibling
        ).start()

    def do_y_last(h):
        if h == 0:
            drain(y_got.at[LAST, 1], ys_s.at[LAST, 1])
            drain(y_last.at[:, 0], g_r.at[LAST, lo])
        drain(y_last.at[pl.ds(0, PIECE), pl.ds(0, 2)], last_r.at[h])
        y_products(LAST, y_last, h * (PIECE // 2), (h + 1) * (PIECE // 2))
        piece = pl.ds(h * PIECE, PIECE)
        remote(
            y_result.at[LAST, 1 - core, piece], y_got.at[LAST, 0, piece], last_ys_s.at[h], last_ys_r.at[h], sibling
        ).start()

    def x_fetch(i, own):
        return pltpu.make_async_copy(x_term.at[(upper if own else 1 - upper) * CHUNKS + i], x_got, x_g)

    def sixteen(ref, j):
        return ref[pl.ds(j * (16 * ZS), 16 * ZS)].reshape(16, ZS, LANES)

    def combine(i, own):
        part, half = (0, lo) if own else (1, other_lo)
        if own:
            x_fetch(i, True).start()

        @pl.loop(0, HALF)
        def _(z):
            turn[pl.ds(core * HALF + z, ROWS, stride=ZS)] = y_result[i, core, z].astype(F32)

        drain(z_out.at[i, half], zo_r.at[i, half])
        z_fetch = pltpu.make_async_copy(z_out.at[i, half], z_got, z_l)
        z_fetch.start()
        drain(y_got.at[i, part], ys_r.at[i, part])

        @pl.loop(0, HALF)
        def _(z):
            turn[pl.ds((1 - core) * HALF + z, ROWS, stride=ZS)] = y_got[i, part, z].astype(F32)

        if own:
            x_fetch(i, True).wait()
        elif i >= 2:
            drain(summed.at[i % 2], back_s.at[i - 2])
        z_fetch.wait()

        @pl.loop(0, ROWS // 16)
        def _(j):
            rows = pl.ds(j * 16, 16)
            both = sixteen(turn, j) + z_got[rows].astype(F32)
            if own:
                total[rows, :, lanes(mine, i)] = (both + sixteen(x_got, j)).astype(BF16)
            else:
                summed[i % 2, rows] = both.astype(BF16)

        if not own:
            remote(summed.at[i % 2], back.at[i], back_s.at[i], back_r.at[i], lo_peer).start()

    def add_last(h, c):
        @pl.loop(h * PIECE, (h + 1) * PIECE)
        def _(z):
            here = pl.ds(c * HALF + z, ROWS, stride=ZS)
            term = y_result[LAST, core, z] if c is core else y_got[LAST, 0, z]
            turn[here] = turn[here] + term.astype(F32)

    def finish_last():
        for h in range(PIECES):
            drain(y_got.at[LAST, 0, pl.ds(0, PIECE)], last_ys_r.at[h])
            add_last(h, other_core)
        drain(z_last, zo_r.at[LAST, lo])

        @pl.loop(0, ROWS // 16)
        def _(j):
            rows = pl.ds(j * 16, 16)
            total[rows, :, lanes(mine, LAST)] = (sixteen(turn, j) + z_last[rows].astype(F32)).astype(BF16)

    def finish(i):
        if i != LAST:
            x_fetch(i, False).start()
        drain(back.at[i], back_r.at[i])
        x_fetch(i, False).wait()

        @pl.loop(0, ROWS // 16)
        def _(j):
            rows = pl.ds(j * 16, 16)
            total[rows, :, lanes(theirs, i)] = (back[i, rows].astype(F32) + sixteen(x_got, j)).astype(BF16)

    def take(i):
        drain(traded.at[i], lo_r.at[i])
        send_z(i, False)
        send_y(i, False)

    for i in range(CHUNKS):
        remote(field.at[:, :, lanes(theirs, i)], traded.at[i], lo_s.at[i], lo_r.at[i], lo_peer).start()
    send_y(0, True)
    send_z(0, True)
    send_z(1, True)
    send_z(2, True)
    for i in range(1, CHUNKS):
        send_y(i, True)
    loads[0].wait()
    do_x(0, 8)
    take(0)
    make_y_op()
    make_z_op()
    do_y(0, False)
    do_x(8, 13)
    take(1)
    do_z(0)
    return_z(0, False)
    send_z(3, True)
    do_y(1, False)
    do_x(13, 18)
    take(2)
    do_z(1)
    return_z(1, False)
    combine(0, False)
    do_y(2, False)
    do_x(18, 21)
    take(3)
    do_z(2)
    return_z(2, False)
    combine(1, False)
    do_x(21, 24)
    do_z(3)
    return_z(3, False)
    for i in range(CHUNKS):
        return_z(i, True)
    for slot in range(2):
        x_store(slot, slot).wait()
    do_y(3, False)
    finish(0)
    do_y(0, True)
    combine(2, False)
    combine(3, False)
    finish(1)
    do_y(1, True)
    combine(0, True)
    finish(2)
    do_y(2, True)
    combine(1, True)
    do_y_last(0)
    combine(2, True)
    x_fetch(LAST, False).start()
    x_last = pltpu.make_async_copy(x_term.at[upper * CHUNKS + LAST], turn.at[pl.ds(0, ROWS * ZS)], load)
    x_last.start()
    x_last.wait()
    add_last(0, core)
    do_y_last(1)
    add_last(1, core)
    do_y_last(2)
    finish(LAST)
    add_last(2, core)
    finish_last()

    for i in range(CHUNKS):
        drain(traded.at[i], lo_s.at[i])
        for part in range(2):
            drain(z_in.at[i, :, pl.ds(0, PLANE - 1), 0], zi_s.at[i, part])
        for n in range(3):
            drain(staged.at[i, pl.ds(0, HALF)], g_s.at[i, 1, n])
        for half in range(2):
            drain(z_out.at[i, half, pl.ds(0, (PLANE - 1) * YS)], zo_s.at[i, half])
        if i != LAST:
            drain(y_got.at[i, 0], ys_s.at[i, 0])
        if i >= 2:
            drain(summed.at[i % 2], back_s.at[i])
    for n in range(PIECES):
        drain(y_got.at[LAST, 0, pl.ds(0, PIECE)], last_ys_s.at[n])


def laplacian(*operands):
    any_space, vmem = pl.BlockSpec(memory_space=pl.ANY), pl.BlockSpec(memory_space=pltpu.VMEM)
    shape = lambda *dims: jax.ShapeDtypeStruct(dims, BF16)
    held = lambda *dims: pltpu.VMEM(dims, BF16)
    dma = pltpu.SemaphoreType.DMA
    nx = 2 * CHUNKS * LANES
    return pl.pallas_call(
        laplacian_kernel,
        name="laplacian",
        out_shape=(
            held(ROWS, ZS, nx),
            shape(CHUNKS, ROWS, ZS, LANES),
            shape(CHUNKS, YS, PLANE, 2, ZS, LANES),
            shape(CHUNKS, 2, HALF, 4, ROWS, LANES),
            shape(CHUNKS, 2, ROWS, ZS, LANES),
            jax.ShapeDtypeStruct((2 * CHUNKS, ROWS * ZS, LANES), F32),
        ),
        in_specs=[any_space] * 4 + [vmem] * 2 + [any_space],
        out_specs=(vmem,) + (any_space,) * 5,
        scratch_shapes=[
            held(nx, nx), held(2, NY, 2 * ROWS), held(2 * ROWS, NY), held(NZ, NZ), held(NZ, NZ),
            held(2, XS, ZS, nx),
            pltpu.VMEM((2, 2 * CHUNKS, XS * ZS, LANES), F32),
            pltpu.VMEM((ROWS * ZS, LANES), F32),
            pltpu.VMEM((ROWS * ZS + ZS, LANES), F32),
            held(CHUNKS, ZS, ROWS, LANES),
            held(ROWS, ZS, LANES),
            held(YS, PLANE, 2, ZS, LANES),
            held(CHUNKS, YS, PLANE, 2, ZS, LANES),
            held(HALF, 4, ROWS, LANES),
            held(CHUNKS, 2, HALF, ROWS, LANES),
            held(CHUNKS, 2, HALF, ROWS, LANES),
            held(ROWS, ZS, LANES),
            held(2, ROWS, ZS, LANES),
            held(CHUNKS, ROWS, ZS, LANES), held(HALF, 4, ROWS, LANES), held(ROWS, ZS, LANES),
            dma((CHUNKS,)), dma((CHUNKS,)),
            dma((CHUNKS, 2)), dma((CHUNKS,)),
            dma((CHUNKS, 2, 3)), dma((CHUNKS, 2)), dma((CHUNKS, 2)),
            dma((CHUNKS, 2)), dma((CHUNKS, 2)),
            dma((CHUNKS, 2)), dma((CHUNKS, 2)),
            dma((CHUNKS,)), dma((CHUNKS,)),
            dma, dma((4,)), dma((2,)), dma((2,)), dma,
            dma, dma((PIECES,)), dma((PIECES,)), dma((PIECES,)),
        ],
        compiler_params=pltpu.CompilerParams(
            collective_id=0, has_side_effects=True, vmem_limit_bytes=54 * 2**20
        ),
        cost_estimate=pl.CostEstimate(flops=24_200_000_000, bytes_accessed=180_000_000, transcendentals=0),
    )(*operands)[0]


def write_kernel(source, target, sems):
    parts = sems.shape[0]
    rows = source.shape[0] // parts
    copies = [
        pltpu.make_async_copy(source.at[pl.ds(n * rows, rows)], target.at[pl.ds(n * rows, rows)], sems.at[n])
        for n in range(parts)
    ]
    for copy in copies:
        copy.start()
    for copy in copies:
        copy.wait()


def written(array):
    return pl.pallas_call(
        write_kernel,
        name="result",
        in_specs=[pl.BlockSpec(memory_space=pltpu.VMEM)],
        out_specs=pl.BlockSpec(memory_space=pl.ANY),
        out_shape=jax.ShapeDtypeStruct(array.shape, array.dtype),
        scratch_shapes=[pltpu.SemaphoreType.DMA((4,))],
        compiler_params=pltpu.CompilerParams(vmem_limit_bytes=16 * 2**20),
    )(array)


def per_device(scalar_field, x_operator, y_second, y_first, y_stretch, y_curve, z_operator):
    return written(laplacian(
        scalar_field, x_operator, y_second, y_first, y_stretch, y_curve, z_operator
    ))


def solution(mesh):
    in_specs = (P("row", "col", None), P(), P(), P(), P(), P(), P())
    out_specs = P("row", "col", None)
    return jax.shard_map(
        per_device, mesh=mesh, in_specs=in_specs, out_specs=out_specs, check_vma=False
    )
```
